512 devices in a mesh: dp: 32 (over z_lo, y), row: 2 (over z_hi), col: 8 (over x, core).
Axes of the slice: x: 4, y: 4, z: 16 (z_hi: 2, z_lo: 8; z = z_hi * 8 + z_lo), core: 2. Of those that a mesh axis runs over, the one named last changes fastest.
Arguments:
- cotangent: bfloat16 [32, 3072, 4096], P('dp', None, ('row', 'col')), may hold values from -1.5 to 1.5
- routed: int32 [32, 768], P('dp'), may hold values from 0 to 3071, as said below
- counts: int32 [32], replicated, may hold values from 0 to 768, as said below
- logits: float32 [32, 768], P('dp'), may hold values from -6 to 6
- query_rows: bfloat16 [32, 768, 4096], P('dp', None, ('row', 'col')), may hold values from -7 to 7
- key_rows: bfloat16 [32, 768, 512], P('dp', None, 'row'), may hold values from -7 to 7
- routed_value_rows: bfloat16 [32, 768, 512], P('dp', None, 'row'), may hold values from -6 to 6
- w_out: bfloat16 [4096, 4096], P(None, ('row', 'col')), may hold values from -0.09375 to 0.09375
Outputs:
- grad_queries: bfloat16 [32, 768, 4096], P('dp', None, ('row', 'col'))
- grad_keys: bfloat16 [32, 768, 512], P('dp', None, 'row')
- grad_values: bfloat16 [32, 768, 512], P('dp', None, 'row')
- grad_w_out: bfloat16 [4096, 4096], P('dp', ('row', 'col'))
- grad_logits: float32 [32, 768], P('dp')
The draws below stay inside these ranges and needn't reach their ends.
Inputs may be any that keep to these rules, and one draw needn't show every extreme that they name: counts[s] of sequence s's 768 slots are routed; the counts of all sequences sum to 12288, and one of them is 768. Each row holds distinct positions; its first counts[s] entries are increasing and are the routed tokens, the later ones are not used.
All inputs are finite; a program needn't handle non-finite values.
Results may differ from the reference program's by a relative error of at most 0.015.
Values may be sent and summed in bfloat16 or wider, within the bound.
No kernel may reach another device: no remote copies, remote signals or barrier semaphores. Data moves between devices by JAX's collectives and lax.ppermute only.
A program may use at most 64 MiB of HBM per device.

```python
import jax
import jax.numpy as jnp
from jax import lax

DW = 4096
QUERY_HEAD_COUNT = 32
KEY_VALUE_HEADS = 4
HEAD_SIZE = 128
SEQ_LEN = 3072
SLOT_CAPACITY = 768
SEQUENCE_COUNT = 32


def routed_counts(key):
    key = jax.random.fold_in(key, 101)
    mean_rows = SEQ_LEN // 8
    cycle_order = jax.random.permutation(jax.random.fold_in(key, 1), SEQUENCE_COUNT)
    amounts = jax.random.randint(jax.random.fold_in(key, 2), (SEQUENCE_COUNT,), 0, mean_rows + 1)
    amounts = amounts.at[0].set(mean_rows).at[1].set(0)
    change = amounts - jnp.roll(amounts, -1)
    return jnp.zeros((SEQUENCE_COUNT,), jnp.int32).at[cycle_order].set((mean_rows + change).astype(jnp.int32))


def draw_counts(key, part):
    shared = routed_counts(key)
    return shared


def draw_routed(key, part):
    shared = routed_counts(key)
    key = jax.random.fold_in(key, 7)
    subkeys = jax.random.split(key, SEQUENCE_COUNT)
    positions = jax.vmap(lambda subkey: jax.random.permutation(subkey, SEQ_LEN)[:SLOT_CAPACITY])(subkeys)
    slot_ids = jnp.arange(SLOT_CAPACITY)
    shifted = jnp.where(slot_ids[None, :] < shared[:, None], positions, positions + SEQ_LEN)
    return (jnp.sort(shifted, axis=1) % SEQ_LEN).astype(jnp.int32)


def draw_query_rows(key, part):
    key = jax.random.fold_in(key, 3)
    sampled_draws = jax.random.truncated_normal(key, -5.0, 5.0, (SEQUENCE_COUNT, SLOT_CAPACITY, QUERY_HEAD_COUNT * HEAD_SIZE), jnp.float32)
    return sampled_draws.astype(jnp.bfloat16)


def draw_key_rows(key, part):
    key = jax.random.fold_in(key, 4)
    sampled_draws = jax.random.truncated_normal(key, -5.0, 5.0, (SEQUENCE_COUNT, SLOT_CAPACITY, KEY_VALUE_HEADS * HEAD_SIZE), jnp.float32)
    return sampled_draws.astype(jnp.bfloat16)


def with_spikes(values, own_key, source, target, parts, factor):
    def block_of(axis_at):
        return (jnp.arange(values.shape[axis_at]) // (values.shape[axis_at] // parts)).reshape((-1,) + (1,) * (values.ndim - 1 - axis_at))

    near = jax.random.permutation(own_key, parts)[block_of(target)]
    second = (block_of(target) + parts // 2) % parts
    return jnp.where((block_of(source) == near) | (block_of(source) == second), factor * values, values)


def level_of(rng, extent, shards, low, top_value):
    def one(position, blocks):
        draws = jax.random.uniform(jax.random.fold_in(jax.random.fold_in(rng, 6), position), (blocks,), jnp.float32, low / len(shards), top_value / len(shards))
        return jnp.repeat(jnp.exp(draws), extent[position] // blocks).reshape((-1,) + (1,) * (len(extent) - position - 1))

    gain = one(*shards[0])
    for cut in shards[1:]:
        gain = gain * one(*cut)
    return gain


def scatter_about(stream_key, dims, scale, bound, shards=(), kind=jnp.bfloat16):
    values = scale * jax.random.normal(stream_key, dims, jnp.float32)
    if shards:
        values = values * level_of(stream_key, dims, shards, -0.22, 0.18)
    return jnp.clip(values, -bound, bound).astype(kind)


def gaussian_with(stream_key, dims, deviation, most, cuts, heavy, held_as=jnp.bfloat16):
    array = deviation * jax.random.normal(stream_key, dims, jnp.float32)
    if cuts:
        array = array * level_of(stream_key, dims, cuts, -0.22, 0.18)
    return jnp.clip(with_spikes(array, jax.random.fold_in(stream_key, 3), *heavy), -most, most).astype(held_as)


def setup_inputs(seed: int = 0) -> dict:
    keys = jax.random.split(jax.random.key(seed), 9)
    cotangent = gaussian_with(keys[0], (SEQUENCE_COUNT, SEQ_LEN, DW), 0.25, 1.5, ((0, 32), (2, 16)), (0, 2, 32, 2.75))
    routed = draw_routed(jax.random.fold_in(keys[8], 71), 0)
    counts = draw_counts(jax.random.fold_in(keys[8], 71), 0)
    logits = scatter_about(keys[3], (SEQUENCE_COUNT, SLOT_CAPACITY), 2.0, 6.0, ((0, 32),), jnp.float32)
    query_rows = draw_query_rows(jax.random.fold_in(keys[8], 71), 0)
    key_rows = draw_key_rows(jax.random.fold_in(keys[8], 71), 0)
    routed_value_rows = scatter_about(keys[6], (SEQUENCE_COUNT, SLOT_CAPACITY, KEY_VALUE_HEADS * HEAD_SIZE), 1.0, 6.0, ((0, 32), (2, 2)))
    w_out = scatter_about(keys[7], (DW, QUERY_HEAD_COUNT * HEAD_SIZE), (QUERY_HEAD_COUNT * HEAD_SIZE) ** -0.5, 0.09375, ((1, 16),))
    return dict(cotangent=cotangent, routed=routed, counts=counts, logits=logits, query_rows=query_rows, key_rows=key_rows, routed_value_rows=routed_value_rows, w_out=w_out)


def reference(cotangent, routed, counts, logits, query_rows, key_rows, routed_value_rows, w_out):
    score_scale = HEAD_SIZE ** -0.5
    group_width = QUERY_HEAD_COUNT // KEY_VALUE_HEADS
    slot_ids = jnp.arange(SLOT_CAPACITY, dtype=jnp.int32)

    def per_sequence(w_grad_sum, inputs):
        grad_seq, positions, own_count, logit_seq, query_seq, key_sequence, value_sequence = inputs
        live_rows = slot_ids < own_count
        picked = jnp.take(grad_seq, positions, axis=0) * live_rows[:, None].astype(grad_seq.dtype)
        router_weight = jax.nn.sigmoid(logit_seq.astype(jnp.float32))
        query_heads = query_seq.reshape(SLOT_CAPACITY, QUERY_HEAD_COUNT, HEAD_SIZE).astype(jnp.float32)
        key_head_rows = jnp.repeat(key_sequence.reshape(SLOT_CAPACITY, KEY_VALUE_HEADS, HEAD_SIZE), group_width, axis=1).astype(jnp.float32)
        value_head_rows = jnp.repeat(value_sequence.reshape(SLOT_CAPACITY, KEY_VALUE_HEADS, HEAD_SIZE), group_width, axis=1).astype(jnp.float32)
        allowed = (live_rows[None, :] & (positions[None, :] <= positions[:, None])) | (slot_ids[:, None] == slot_ids[None, :])
        scores = jnp.einsum("ihd,jhd->hij", query_heads, key_head_rows) * score_scale
        scores = jnp.where(allowed[None], scores, -jnp.inf)
        scores = scores - jnp.max(scores, axis=2, keepdims=True)
        exponent = jnp.exp(scores)
        attn_probs = exponent / jnp.sum(exponent, axis=2, keepdims=True)
        probs_rounded = lax.optimization_barrier(attn_probs.astype(jnp.bfloat16)).astype(jnp.float32)
        attended = jnp.einsum("hij,jhd->ihd", probs_rounded, value_head_rows).reshape(SLOT_CAPACITY, QUERY_HEAD_COUNT * HEAD_SIZE).astype(jnp.bfloat16)
        attended_wide = lax.optimization_barrier(attended).astype(jnp.float32)
        scaled = (router_weight[:, None] * attended_wide).astype(jnp.bfloat16)
        grad_o = jnp.dot(picked, w_out, preferred_element_type=jnp.float32)
        w_grad_sum = w_grad_sum + jnp.dot(picked.T, scaled, preferred_element_type=jnp.float32)
        router_grad = jnp.sum(grad_o * attended_wide, axis=1)
        grad_logits = router_grad * router_weight * (1.0 - router_weight)
        grad_attn = lax.optimization_barrier((router_weight[:, None] * grad_o).astype(jnp.bfloat16))
        grad_attn = grad_attn.astype(jnp.float32).reshape(SLOT_CAPACITY, QUERY_HEAD_COUNT, HEAD_SIZE)
        value_portion = jnp.einsum("hij,ihd->jhd", probs_rounded, grad_attn)
        grad_probs = jnp.einsum("ihd,jhd->hij", grad_attn, value_head_rows)
        row_delta = jnp.sum(attn_probs * grad_probs, axis=2, keepdims=True)
        grad_scores = lax.optimization_barrier((attn_probs * (grad_probs - row_delta)).astype(jnp.bfloat16)).astype(jnp.float32)
        grad_q = (jnp.einsum("hij,jhd->ihd", grad_scores, key_head_rows) * score_scale).reshape(SLOT_CAPACITY, QUERY_HEAD_COUNT * HEAD_SIZE).astype(jnp.bfloat16)
        key_portion = jnp.einsum("hij,ihd->jhd", grad_scores, query_heads) * score_scale
        key_gradient = key_portion.reshape(SLOT_CAPACITY, KEY_VALUE_HEADS, group_width, HEAD_SIZE).sum(axis=2).reshape(SLOT_CAPACITY, KEY_VALUE_HEADS * HEAD_SIZE).astype(jnp.bfloat16)
        value_gradient = value_portion.reshape(SLOT_CAPACITY, KEY_VALUE_HEADS, group_width, HEAD_SIZE).sum(axis=2).reshape(SLOT_CAPACITY, KEY_VALUE_HEADS * HEAD_SIZE).astype(jnp.bfloat16)
        return w_grad_sum, (grad_q, key_gradient, value_gradient, grad_logits)

    start_sum = jnp.zeros((DW, QUERY_HEAD_COUNT * HEAD_SIZE), jnp.float32)
    w_grad_sum, outputs = lax.scan(per_sequence, start_sum, (cotangent, routed, counts, logits, query_rows, key_rows, routed_value_rows))
    grad_queries, grad_keys, grad_values, grad_logits = outputs
    return (grad_queries, grad_keys, grad_values, w_grad_sum.astype(jnp.bfloat16), grad_logits)
```

```python
import jax
import jax.numpy as jnp
from jax import lax
from jax.sharding import Mesh
from jax.sharding import PartitionSpec as P

QUERY_HEAD_COUNT = 32
KEY_VALUE_HEADS = 4
HEAD_SIZE = 128
ZL, Y, ZH, X, CORE = 8, 4, 2, 4, 2


def ring(n, k):
    return [(i, (i + k) % n) for i in range(n)]


def swap(value, axis):
    return lax.ppermute(value, axis, ring(2, 1))


def gather_x(block):
    copies = jnp.broadcast_to(block[None], (X,) + block.shape)
    return lax.all_to_all(copies, "x", 0, 0, tiled=True)


def attention_parts(positions, live_rows, query_heads, key_head, value_head):
    slot_ids = jnp.arange(positions.shape[0], dtype=jnp.int32)
    allowed = live_rows[None, :] & (positions[None, :] <= positions[:, None]) | (
        slot_ids[:, None] == slot_ids[None, :]
    )
    scores = jnp.einsum("ihd,jd->hij", query_heads, key_head, preferred_element_type=jnp.float32)
    scores = jnp.where(allowed[None], scores * HEAD_SIZE ** (-0.5), -jnp.inf)
    exponent = jnp.exp(scores - jnp.max(scores, axis=2, keepdims=True))
    return exponent / jnp.sum(exponent, axis=2, keepdims=True)


def half_products(near, far, w_half, scaled, core):
    both = jnp.where(core == 0, jnp.stack([near, far], 1), jnp.stack([far, near], 1))
    grad_o = jnp.einsum("xqif,xqfc->ic", both, w_half, preferred_element_type=jnp.float32)
    w_grad = jnp.einsum("xqif,ic->qfxc", both, scaled, preferred_element_type=jnp.float32)
    w_grad = w_grad.astype(jnp.bfloat16).reshape(CORE, 2, 128, X, 256).transpose(0, 1, 3, 2, 4)
    return grad_o, w_grad.reshape(Y, X, 128, 256)


def sum_over_y(blocks):
    moved = lax.all_to_all(blocks, "y", 0, 0, tiled=True)
    return jnp.sum(moved.astype(jnp.float32), axis=0).astype(jnp.bfloat16)


def per_device(cotangent, routed, counts, logits, query_rows, key_rows, routed_value_rows, w_out):
    slot_total = routed.shape[1]
    zh, x, core = lax.axis_index("zh"), lax.axis_index("x"), lax.axis_index("core")
    dp_index = lax.axis_index("zl") * Y + lax.axis_index("y")
    own_count = lax.dynamic_index_in_dim(counts, dp_index, 0, keepdims=False)
    live_rows = jnp.arange(slot_total, dtype=jnp.int32) < own_count
    positions = routed[0]
    picked = jnp.take(cotangent[0], positions, axis=0) * live_rows[:, None].astype(cotangent.dtype)
    other_picked = swap(picked, "zh")
    own_near = gather_x(picked)
    own_far = swap(own_near, "core")

    router_weight = jax.nn.sigmoid(logits[0])
    heads = query_rows.shape[2] // HEAD_SIZE
    group = x // 2
    query_heads = query_rows[0].reshape(slot_total, heads, HEAD_SIZE)
    key_head = lax.dynamic_slice_in_dim(key_rows[0], group * HEAD_SIZE, HEAD_SIZE, 1)
    value_head = lax.dynamic_slice_in_dim(routed_value_rows[0], group * HEAD_SIZE, HEAD_SIZE, 1)
    attn_probs = attention_parts(positions, live_rows, query_heads, key_head, value_head)
    probs_rounded = attn_probs.astype(jnp.bfloat16)
    attended = jnp.einsum(
        "hij,jd->ihd", probs_rounded, value_head, preferred_element_type=jnp.float32
    )
    attended_wide = attended.astype(jnp.bfloat16).reshape(slot_total, -1).astype(jnp.float32)
    scaled = (router_weight[:, None] * attended_wide).astype(jnp.bfloat16)

    w_parts = w_out.reshape(ZH, X, CORE, 256, 256)
    w_own = lax.dynamic_index_in_dim(w_parts, zh, 0, keepdims=False)
    w_other = lax.dynamic_index_in_dim(w_parts, 1 - zh, 0, keepdims=False)
    grad_o_own, w_grad_own = half_products(own_near, own_far, w_own, scaled, core)
    y_own = sum_over_y(w_grad_own)

    other_near = gather_x(other_picked)
    other_far = swap(other_near, "core")
    grad_o_other, w_grad_other = half_products(other_near, other_far, w_other, scaled, core)
    grad_o = grad_o_own + grad_o_other
    y_other = sum_over_y(w_grad_other)

    router = jnp.sum(grad_o * attended_wide, axis=1)
    grad_attn = (
        (router_weight[:, None] * grad_o)
        .astype(jnp.bfloat16)
        .reshape(slot_total, heads, HEAD_SIZE)
    )
    value_part = jnp.einsum(
        "hij,ihd->jd", probs_rounded, grad_attn, preferred_element_type=jnp.float32
    )
    grad_probs = jnp.einsum(
        "ihd,jd->hij", grad_attn, value_head, preferred_element_type=jnp.float32
    )
    row_delta = jnp.sum(attn_probs * grad_probs, axis=2, keepdims=True)
    grad_scores = (attn_probs * (grad_probs - row_delta)).astype(jnp.bfloat16)
    score_scale = HEAD_SIZE ** (-0.5)
    grad_q = (
        jnp.einsum("hij,jd->ihd", grad_scores, key_head, preferred_element_type=jnp.float32)
        * score_scale
    )
    grad_q = grad_q.astype(jnp.bfloat16).reshape(slot_total, -1)
    key_part = (
        jnp.einsum("hij,ihd->jd", grad_scores, query_heads, preferred_element_type=jnp.float32)
        * score_scale
    )

    half = slot_total // 2
    kv = jnp.concatenate([key_part, value_part], axis=1)
    kept = lax.dynamic_slice_in_dim(kv, core * half, half, 0)
    sent = lax.dynamic_slice_in_dim(kv, (1 - core) * half, half, 0).astype(jnp.bfloat16)
    chip = (kept + swap(sent, "core").astype(jnp.float32)).astype(jnp.bfloat16)
    router = router + swap(router, "core")
    pieces = [(x, chip)] + [
        ((x - k) % X, lax.ppermute(chip, "x", ring(X, k))) for k in (1, 3, 2)
    ]
    router = router + lax.ppermute(router, "x", ring(X, 1))
    router = router + lax.ppermute(router, "x", ring(X, 2))
    router = router + swap(router, "zh")
    totals = []
    for g in range(2):
        totals.append(
            sum(jnp.where(src // 2 == g, piece.astype(jnp.float32), 0.0) for src, piece in pieces)
        )
    joined = jnp.stack(totals, axis=1).reshape(half, 2, 2, HEAD_SIZE)
    joined = joined.transpose(0, 2, 1, 3).reshape(half, 4 * HEAD_SIZE).astype(jnp.bfloat16)
    theirs = swap(joined, "core")
    rows = jnp.where(
        core == 0, jnp.concatenate([joined, theirs], 0), jnp.concatenate([theirs, joined], 0)
    )
    key_total, value_total = rows[:, : 2 * HEAD_SIZE], rows[:, 2 * HEAD_SIZE :]

    blocks = jnp.where(
        zh == 0, jnp.concatenate([y_own, y_other], 0), jnp.concatenate([y_other, y_own], 0)
    )
    moved = lax.all_to_all(blocks, "zl", 0, 0, tiled=True)
    w_grad = jnp.sum(moved.astype(jnp.float32), axis=0).astype(jnp.bfloat16)

    grad_logits = router * router_weight * (1.0 - router_weight)
    return (grad_q[None], key_total[None], value_total[None], w_grad, grad_logits[None])


def solution(mesh):
    fine = Mesh(mesh.devices.reshape(ZL, Y, ZH, X, CORE), ("zl", "y", "zh", "x", "core"))
    dp, col = ("zl", "y"), ("x", "core")
    row_col = ("zh",) + col
    placed = (
        P(dp, None, row_col),
        P(dp, None),
        P(),
        P(dp, None),
        P(dp, None, row_col),
        P(dp, None, "zh"),
        P(dp, None, "zh"),
        P(None, row_col),
    )
    return jax.shard_map(
        per_device,
        mesh=fine,
        in_specs=placed,
        out_specs=(
            P(dp, None, row_col),
            P(dp, None, "zh"),
            P(dp, None, "zh"),
            P(dp, row_col),
            P(dp, None),
        ),
        check_vma=False,
    )
```

```python
import functools

import jax
import jax.numpy as jnp
from jax import lax
from jax.experimental import pallas as pl
from jax.experimental.pallas import tpu as pltpu
from jax.sharding import Mesh
from jax.sharding import PartitionSpec as P

HEAD_SIZE = 128
ZL, Y, ZH, X, CORE = 8, 4, 2, 4, 2
SLOTS, WIDE, HEADS = 768, 256, 2
SCALE = HEAD_SIZE ** (-0.5)
BF, F32 = jnp.bfloat16, jnp.float32
ROWS = 256
STEP = 192
EXTRA = 16
LIMIT = pltpu.CompilerParams(vmem_limit_bytes=40 * 1024 * 1024)


def ring(n, k):
    return [(i, (i + k) % n) for i in range(n)]


def swap(value, axis):
    return lax.ppermute(value, axis, ring(2, 1))


def spread_x(copies):
    return lax.all_to_all(copies, "x", 0, 0, tiled=True)


def repeated(block):
    return jnp.broadcast_to(block[None], (X,) + block.shape)


def exchange(rows, picked):
    other = swap(picked[:rows], "zh")
    near = spread_x(repeated(picked))
    far = swap(near, "core")
    other = jnp.pad(other, ((0, SLOTS - rows), (0, 0)))
    return repeated(other), near, far


def transposed_dot(a, b):
    return lax.dot_general(a, b, (((0,), (0,)), ((), ())), preferred_element_type=F32)


def rows_dot(a, b):
    return lax.dot_general(a, b, (((1,), (1,)), ((), ())), preferred_element_type=F32)


def allowed_block(info_ref, pos_col, pos_row):
    first = pl.program_id(0) * ROWS
    shape = (ROWS, SLOTS)
    i = lax.broadcasted_iota(jnp.int32, shape, 0) + first
    j = lax.broadcasted_iota(jnp.int32, shape, 1)
    return ((j < info_ref[1]) & (pos_row <= pos_col)) | (i == j)


def forward_kernel(info_ref, q_ref, k_ref, v_ref, col_ref, row_ref, logit_ref, att_ref, scaled_ref, lse_ref):
    allowed = allowed_block(info_ref, col_ref[...], row_ref[...])
    weight = 1.0 / (1.0 + jnp.exp(-logit_ref[...]))
    for h in range(HEADS):
        lanes = slice(h * HEAD_SIZE, (h + 1) * HEAD_SIZE)
        s = rows_dot(q_ref[:, lanes], k_ref[...]) * SCALE
        s = jnp.where(allowed, s, -1e30)
        top = jnp.max(s, axis=1, keepdims=True)
        e = jnp.exp(s - top)
        total = jnp.sum(e, axis=1, keepdims=True)
        p = (e * (1.0 / total)).astype(BF)
        att = jnp.dot(p, v_ref[...], preferred_element_type=F32).astype(BF)
        att_ref[:, lanes] = att
        scaled_ref[:, lanes] = (weight * att.astype(F32)).astype(BF)
        lse_ref[:, h : h + 1] = top + jnp.log(total)


def backward_kernel(
    info_ref, q_ref, k_ref, v_ref, col_ref, row_ref, logit_ref, lse_ref, att_ref, go_ref,
    gq_ref, kv_ref, router_ref, sum_ref,
):
    step = pl.program_id(0)
    allowed = allowed_block(info_ref, col_ref[...], row_ref[...])
    weight = 1.0 / (1.0 + jnp.exp(-logit_ref[...]))
    grad_o = go_ref[...]
    router_ref[...] = jnp.sum(grad_o * att_ref[...].astype(F32), axis=1, keepdims=True)
    grad_attn = (weight * grad_o).astype(BF)

    @pl.when(step == 0)
    def _():
        sum_ref[...] = jnp.zeros_like(sum_ref)

    for h in range(HEADS):
        lanes = slice(h * HEAD_SIZE, (h + 1) * HEAD_SIZE)
        q = q_ref[:, lanes]
        s = rows_dot(q, k_ref[...]) * SCALE
        p = jnp.exp(jnp.where(allowed, s - lse_ref[:, h : h + 1], -1e30))
        ga = grad_attn[:, lanes]
        gp = rows_dot(ga, v_ref[...])
        delta = jnp.sum(p * gp, axis=1, keepdims=True)
        gs = (p * (gp - delta)).astype(BF)
        gq = jnp.dot(gs, k_ref[...], preferred_element_type=F32) * SCALE
        gq_ref[:, lanes] = gq.astype(BF)
        sum_ref[:, :HEAD_SIZE] += transposed_dot(gs, q)
        sum_ref[:, HEAD_SIZE:] += transposed_dot(p.astype(BF), ga)

    @pl.when(step == pl.num_programs(0) - 1)
    def _():
        kv_ref[:, :HEAD_SIZE] = (sum_ref[:, :HEAD_SIZE] * SCALE).astype(BF)
        kv_ref[:, HEAD_SIZE:] = sum_ref[:, HEAD_SIZE:].astype(BF)


def by_rows(width):
    return pl.BlockSpec((ROWS, width), lambda i, info: (i, 0))


def by_group():
    return pl.BlockSpec((SLOTS, HEAD_SIZE), lambda i, info: (0, info[0]))


def whole(shape):
    return pl.BlockSpec(shape, lambda i, info: (0,) * len(shape))


def shape_of(shape, dtype):
    return jax.ShapeDtypeStruct(shape, dtype)


def forward(info, q, k, v, pos_col, pos_row, logit_col):
    return pl.pallas_call(
        forward_kernel,
        grid_spec=pltpu.PrefetchScalarGridSpec(
            num_scalar_prefetch=1,
            grid=(SLOTS // ROWS,),
            in_specs=[by_rows(WIDE), by_group(), by_group(), by_rows(1), whole((1, SLOTS)), by_rows(1)],
            out_specs=[by_rows(WIDE), by_rows(WIDE), by_rows(HEADS)],
        ),
        out_shape=[shape_of((SLOTS, WIDE), BF), shape_of((SLOTS, WIDE), BF), shape_of((SLOTS, HEADS), F32)],
        compiler_params=LIMIT,
        cost_estimate=pl.CostEstimate(flops=604 * 10**6, bytes_accessed=2 * 10**6, transcendentals=1200000),
    )(info, q, k, v, pos_col, pos_row, logit_col)


def backward(info, q, k, v, pos_col, pos_row, logit_col, lse, att, grad_o):
    return pl.pallas_call(
        backward_kernel,
        grid_spec=pltpu.PrefetchScalarGridSpec(
            num_scalar_prefetch=1,
            grid=(SLOTS // ROWS,),
            in_specs=[
                by_rows(WIDE), by_group(), by_group(), by_rows(1), whole((1, SLOTS)), by_rows(1),
                by_rows(HEADS), by_rows(WIDE), by_rows(WIDE),
            ],
            out_specs=[by_rows(WIDE), whole((SLOTS, WIDE)), by_rows(1)],
            scratch_shapes=[pltpu.VMEM((SLOTS, WIDE), F32)],
        ),
        out_shape=[shape_of((SLOTS, WIDE), BF), shape_of((SLOTS, WIDE), BF), shape_of((SLOTS, 1), F32)],
        compiler_params=LIMIT,
        cost_estimate=pl.CostEstimate(flops=1510 * 10**6, bytes_accessed=4 * 10**6, transcendentals=1200000),
    )(info, q, k, v, pos_col, pos_row, logit_col, lse, att, grad_o)


def products_kernel(info_ref, near_ref, far_ref, wn_ref, wf_ref, scaled_ref, *refs):
    go_ref, wg_ref = refs[-2:]
    core = info_ref[0]
    near, far, scaled = near_ref[0], far_ref[0], scaled_ref[...]
    part = jnp.dot(near, wn_ref[0], preferred_element_type=F32)
    part = part + jnp.dot(far, wf_ref[0], preferred_element_type=F32)
    first = pl.program_id(0) == 0

    @pl.when(first)
    def _():
        go_ref[...] = part + refs[0][...] if len(refs) == 3 else part

    @pl.when(jnp.logical_not(first))
    def _():
        go_ref[...] += part

    wg_ref[pl.ds(2 * core, 2), 0] = transposed_dot(near, scaled).astype(BF).reshape(2, 128, WIDE)
    wg_ref[pl.ds(2 - 2 * core, 2), 0] = transposed_dot(far, scaled).astype(BF).reshape(2, 128, WIDE)


def products(core, half, near, far, w_out, scaled, begin=None):
    info = jnp.stack([core, half]).astype(jnp.int32)
    shard = pl.BlockSpec((1, SLOTS, WIDE), lambda i, info: (i, 0, 0))
    w_near = pl.BlockSpec((1, WIDE, WIDE), lambda i, info: (info[1] * 8 + i * 2 + info[0], 0, 0))
    w_far = pl.BlockSpec((1, WIDE, WIDE), lambda i, info: (info[1] * 8 + i * 2 + 1 - info[0], 0, 0))
    w_parts = w_out.reshape(ZH * X * CORE, WIDE, WIDE)
    more = [] if begin is None else [begin]
    return pl.pallas_call(
        products_kernel,
        grid_spec=pltpu.PrefetchScalarGridSpec(
            num_scalar_prefetch=1,
            grid=(X,),
            in_specs=[shard, shard, w_near, w_far, whole((SLOTS, WIDE))] + [whole((SLOTS, WIDE)) for _ in more],
            out_specs=[
                whole((SLOTS, WIDE)),
                pl.BlockSpec((Y, 1, 128, WIDE), lambda i, info: (0, i, 0, 0)),
            ],
        ),
        out_shape=[shape_of((SLOTS, WIDE), F32), shape_of((Y, X, 128, WIDE), BF)],
        compiler_params=LIMIT,
        cost_estimate=pl.CostEstimate(flops=1610 * 10**6, bytes_accessed=7 * 10**6, transcendentals=0),
    )(info, near, far, w_parts, w_parts, scaled, *more)


def fold_kernel(info_ref, moved_ref, *refs):
    refs[-1][0] = jnp.sum(moved_ref[...].astype(F32), axis=0)[0].astype(BF)


def fold(half, moved, begin=None):
    more = [] if begin is None else [begin]
    return pl.pallas_call(
        fold_kernel,
        grid_spec=pltpu.PrefetchScalarGridSpec(
            num_scalar_prefetch=1,
            grid=(X,),
            in_specs=[pl.BlockSpec((Y, 1, 128, WIDE), lambda i, info: (0, i, 0, 0))]
            + [pl.BlockSpec(memory_space=pl.ANY) for _ in more],
            out_specs=pl.BlockSpec((1, 128, WIDE), lambda i, info: (info[0] * 4 + i, 0, 0)),
        ),
        out_shape=shape_of((ZL, 128, WIDE), BF),
        input_output_aliases={2: 0} if more else {},
        compiler_params=LIMIT,
        cost_estimate=pl.CostEstimate(flops=4 * 10**6, bytes_accessed=3 * 10**6, transcendentals=0),
    )(half.astype(jnp.int32).reshape(1), moved, *more)


def over_y(blocks):
    return lax.all_to_all(blocks, "y", 0, 0, tiled=True)


def packed(router):
    lead = lax.reduce_precision(router, 8, 7)
    terms = jnp.concatenate([lead, router - lead]).astype(BF).reshape(-1, WIDE)
    return jnp.pad(terms, ((0, EXTRA - terms.shape[0]), (0, 0)))


def unpacked(rows):
    terms = rows[: 2 * SLOTS // WIDE].astype(F32).reshape(2, SLOTS)
    return terms[0] + terms[1]


def per_device(cotangent, routed, counts, logits, query_rows, key_rows, routed_value_rows, w_out):
    zh, x, core = lax.axis_index("zh"), lax.axis_index("x"), lax.axis_index("core")
    dp_index = lax.axis_index("zl") * Y + lax.axis_index("y")
    own = jnp.arange(counts.shape[0], dtype=jnp.int32) == dp_index
    own_count = jnp.sum(jnp.where(own, counts, 0))
    live_rows = jnp.arange(SLOTS, dtype=jnp.int32) < own_count
    positions = routed[0]
    picked = cotangent[0].at[positions].get(mode="promise_in_bounds")
    picked = jnp.where(live_rows[:, None], picked, jnp.zeros((), BF))

    sizes = range(STEP, SLOTS + 1, STEP)
    branch = jnp.maximum(own_count - 1, 0) // STEP
    other_copies, own_near, own_far = lax.switch(
        branch, [functools.partial(exchange, rows) for rows in sizes], picked
    )
    other_near = spread_x(other_copies)

    info = jnp.stack([x // 2, own_count]).astype(jnp.int32)
    attention = (
        info, query_rows[0], key_rows[0], routed_value_rows[0],
        positions[:, None], positions[None, :], logits[0][:, None],
    )
    attended, scaled, lse = forward(*attention)
    grad_o_own, w_grad_own = products(core, zh, own_near, own_far, w_out, scaled)
    blocks = fold(zh, over_y(w_grad_own))

    other_far = swap(other_near, "core")
    grad_o, w_grad_other = products(core, 1 - zh, other_near, other_far, w_out, scaled, grad_o_own)
    moved_other = over_y(w_grad_other)

    grad_q, kv, router = backward(*attention, lse, attended, grad_o)
    router = router[:, 0]
    half = SLOTS // 2
    kept = lax.dynamic_slice_in_dim(kv, core * half, half, 0)
    sent = lax.dynamic_slice_in_dim(kv, (1 - core) * half, half, 0)
    came = swap(jnp.concatenate([sent, packed(router)], 0), "core")
    chip = (kept.astype(F32) + came[:half].astype(F32)).astype(BF)
    router = router + unpacked(came[half:])
    pieces = spread_x(repeated(jnp.concatenate([chip, packed(router)], 0)))

    blocks = fold(1 - zh, moved_other, blocks)
    final = lax.all_to_all(blocks, "zl", 0, 0, tiled=True)
    w_grad = jnp.sum(final.astype(F32), axis=0).astype(BF)

    wide = pieces[:, :half].astype(F32)
    first, second = wide[0] + wide[1], wide[2] + wide[3]
    joined = jnp.concatenate(
        [first[:, :HEAD_SIZE], second[:, :HEAD_SIZE], first[:, HEAD_SIZE:], second[:, HEAD_SIZE:]], 1
    ).astype(BF)
    theirs = swap(joined, "core")
    router = sum(unpacked(pieces[s, half:]) for s in range(X))
    router = router + swap(router, "zh")
    rows = jnp.where(
        core == 0, jnp.concatenate([joined, theirs], 0), jnp.concatenate([theirs, joined], 0)
    )
    key_total, value_total = rows[:, : 2 * HEAD_SIZE], rows[:, 2 * HEAD_SIZE :]
    router_weight = jax.nn.sigmoid(logits[0])
    grad_logits = router * router_weight * (1.0 - router_weight)
    return (grad_q[None], key_total[None], value_total[None], w_grad, grad_logits[None])


def solution(mesh):
    fine = Mesh(mesh.devices.reshape(ZL, Y, ZH, X, CORE), ("zl", "y", "zh", "x", "core"))
    dp, col = ("zl", "y"), ("x", "core")
    row_col = ("zh",) + col
    placed = (
        P(dp, None, row_col),
        P(dp, None),
        P(),
        P(dp, None),
        P(dp, None, row_col),
        P(dp, None, "zh"),
        P(dp, None, "zh"),
        P(None, row_col),
    )
    return jax.shard_map(
        per_device,
        mesh=fine,
        in_specs=placed,
        out_specs=(
            P(dp, None, row_col),
            P(dp, None, "zh"),
            P(dp, None, "zh"),
            P(dp, row_col),
            P(dp, None),
        ),
        check_vma=False,
    )
```

```python
import functools

import jax
import jax.numpy as jnp
from jax import lax
from jax.experimental import pallas as pl
from jax.experimental.pallas import tpu as pltpu
from jax.sharding import Mesh
from jax.sharding import PartitionSpec as P

HEAD_SIZE = 128
ZQ, ZP, Y, ZH, X, CORE = 4, 2, 4, 2, 4, 2
SLOTS, WIDE, HEADS = 768, 256, 2
SCALE = HEAD_SIZE ** (-0.5)
BF, F32 = jnp.bfloat16, jnp.float32
ROWS = 256
STEP = 64
EXTRA = 16
LIMIT = pltpu.CompilerParams(vmem_limit_bytes=60 * 1024 * 1024)


def ring(n, k):
    return [(i, (i + k) % n) for i in range(n)]


def swap(value, axis):
    return lax.ppermute(value, axis, ring(2, 1))


def spread_x(copies):
    return lax.all_to_all(copies, "x", 0, 0, tiled=True)


def repeated(block):
    return jnp.broadcast_to(block[None], (X,) + block.shape)


def exchange(rows, copies):
    other = swap(copies[0, :rows], "zh")
    near = spread_x(copies)
    other = jnp.pad(other, ((0, SLOTS - rows), (0, 0)))
    return repeated(other), near


def transposed_dot(a, b):
    return lax.dot_general(a, b, (((0,), (0,)), ((), ())), preferred_element_type=F32)


def rows_dot(a, b):
    return lax.dot_general(a, b, (((1,), (1,)), ((), ())), preferred_element_type=F32)


def allowed_block(info_ref, pos_col, pos_row):
    first = pl.program_id(0) * ROWS
    shape = (ROWS, SLOTS)
    i = lax.broadcasted_iota(jnp.int32, shape, 0) + first
    j = lax.broadcasted_iota(jnp.int32, shape, 1)
    return ((j < info_ref[1]) & (pos_row <= pos_col)) | (i == j)


def forward_kernel(info_ref, q_ref, k_ref, v_ref, col_ref, row_ref, logit_ref, att_ref, scaled_ref, lse_ref):
    allowed = allowed_block(info_ref, col_ref[...], row_ref[...])
    weight = 1.0 / (1.0 + jnp.exp(-logit_ref[...]))
    for h in range(HEADS):
        lanes = slice(h * HEAD_SIZE, (h + 1) * HEAD_SIZE)
        s = rows_dot(q_ref[:, lanes], k_ref[...]) * SCALE
        s = jnp.where(allowed, s, -1e30)
        top = jnp.max(s, axis=1, keepdims=True)
        e = jnp.exp(s - top)
        total = jnp.sum(e, axis=1, keepdims=True)
        p = (e * (1.0 / total)).astype(BF)
        att = jnp.dot(p, v_ref[...], preferred_element_type=F32).astype(BF)
        att_ref[:, lanes] = att
        scaled_ref[lanes, :] = (weight * att.astype(F32)).astype(BF).T
        lse_ref[:, h : h + 1] = top + jnp.log(total)


def backward_kernel(
    info_ref, q_ref, k_ref, v_ref, col_ref, row_ref, logit_ref, lse_ref, att_ref, go_ref,
    gq_ref, kv_ref, router_ref, sum_ref,
):
    step = pl.program_id(0)
    allowed = allowed_block(info_ref, col_ref[...], row_ref[...])
    weight = 1.0 / (1.0 + jnp.exp(-logit_ref[...]))
    grad_o = go_ref[...]
    router_ref[...] = jnp.sum(grad_o * att_ref[...].astype(F32), axis=1, keepdims=True)
    grad_attn = (weight * grad_o).astype(BF)

    @pl.when(step == 0)
    def _():
        sum_ref[...] = jnp.zeros_like(sum_ref)

    for h in range(HEADS):
        lanes = slice(h * HEAD_SIZE, (h + 1) * HEAD_SIZE)
        q = q_ref[:, lanes]
        s = rows_dot(q, k_ref[...]) * SCALE
        p = jnp.exp(jnp.where(allowed, s - lse_ref[:, h : h + 1], -1e30))
        ga = grad_attn[:, lanes]
        gp = rows_dot(ga, v_ref[...])
        delta = jnp.sum(p * gp, axis=1, keepdims=True)
        gs = (p * (gp - delta)).astype(BF)
        gq = jnp.dot(gs, k_ref[...], preferred_element_type=F32) * SCALE
        gq_ref[:, lanes] = gq.astype(BF)
        sum_ref[:, :HEAD_SIZE] += transposed_dot(gs, q)
        sum_ref[:, HEAD_SIZE:] += transposed_dot(p.astype(BF), ga)

    @pl.when(step == pl.num_programs(0) - 1)
    def _():
        kv_ref[:, :HEAD_SIZE] = (sum_ref[:, :HEAD_SIZE] * SCALE).astype(BF)
        kv_ref[:, HEAD_SIZE:] = sum_ref[:, HEAD_SIZE:].astype(BF)


def by_rows(width):
    return pl.BlockSpec((ROWS, width), lambda i, info: (i, 0))


def by_group():
    return pl.BlockSpec((SLOTS, HEAD_SIZE), lambda i, info: (0, info[0]))


def whole(shape):
    return pl.BlockSpec(shape, lambda i, info: (0,) * len(shape))


def shape_of(shape, dtype):
    return jax.ShapeDtypeStruct(shape, dtype)


def forward(info, q, k, v, pos_col, pos_row, logit_col):
    return pl.pallas_call(
        forward_kernel,
        grid_spec=pltpu.PrefetchScalarGridSpec(
            num_scalar_prefetch=1,
            grid=(SLOTS // ROWS,),
            in_specs=[by_rows(WIDE), by_group(), by_group(), by_rows(1), whole((1, SLOTS)), by_rows(1)],
            out_specs=[by_rows(WIDE), pl.BlockSpec((WIDE, ROWS), lambda i, info: (0, i)), by_rows(HEADS)],
        ),
        out_shape=[shape_of((SLOTS, WIDE), BF), shape_of((WIDE, SLOTS), BF), shape_of((SLOTS, HEADS), F32)],
        compiler_params=LIMIT,
        cost_estimate=pl.CostEstimate(flops=604 * 10**6, bytes_accessed=2 * 10**6, transcendentals=1200000),
    )(info, q, k, v, pos_col, pos_row, logit_col)


def backward(info, q, k, v, pos_col, pos_row, logit_col, lse, att, grad_o):
    return pl.pallas_call(
        backward_kernel,
        grid_spec=pltpu.PrefetchScalarGridSpec(
            num_scalar_prefetch=1,
            grid=(SLOTS // ROWS,),
            in_specs=[
                by_rows(WIDE), by_group(), by_group(), by_rows(1), whole((1, SLOTS)), by_rows(1),
                by_rows(HEADS), by_rows(WIDE), by_rows(WIDE),
            ],
            out_specs=[by_rows(WIDE), whole((SLOTS, WIDE)), by_rows(1)],
            scratch_shapes=[pltpu.VMEM((SLOTS, WIDE), F32)],
        ),
        out_shape=[shape_of((SLOTS, WIDE), BF), shape_of((SLOTS, WIDE), BF), shape_of((SLOTS, 1), F32)],
        compiler_params=LIMIT,
        cost_estimate=pl.CostEstimate(flops=1510 * 10**6, bytes_accessed=4 * 10**6, transcendentals=1200000),
    )(info, q, k, v, pos_col, pos_row, logit_col, lse, att, grad_o)


def products_kernel(info_ref, shard_ref, w_ref, scaled_ref, *refs):
    go_ref, wg_ref = refs[-2:]
    shard = shard_ref[0]
    part = jnp.dot(shard, w_ref[0], preferred_element_type=F32)
    first = pl.program_id(0) == 0

    @pl.when(first)
    def _():
        go_ref[...] = part + refs[0][...] if len(refs) > 2 else part

    @pl.when(jnp.logical_not(first))
    def _():
        go_ref[...] += part

    grad = jnp.dot(scaled_ref[...], shard, preferred_element_type=F32).astype(BF)
    wg_ref[0, 0, 0] = grad[:, :128]
    wg_ref[0, 1, 0] = grad[:, 128:]


def products(core, half, shards, w_out, scaled_t, grad_o=None, blocks=None):
    info = jnp.stack([core, half]).astype(jnp.int32)
    more, more_specs, aliases = [], [], {}
    if grad_o is not None:
        more, more_specs = [grad_o], [whole((SLOTS, WIDE))]
    if blocks is not None:
        aliases = {4 + len(more): 1}
        more, more_specs = more + [blocks], more_specs + [pl.BlockSpec(memory_space=pl.ANY)]
    return pl.pallas_call(
        products_kernel,
        grid_spec=pltpu.PrefetchScalarGridSpec(
            num_scalar_prefetch=1,
            grid=(X,),
            in_specs=[
                pl.BlockSpec((1, SLOTS, WIDE), lambda i, info: (i, 0, 0)),
                pl.BlockSpec((1, WIDE, WIDE), lambda i, info: (info[1] * 8 + i * 2 + info[0], 0, 0)),
                whole((WIDE, SLOTS)),
            ]
            + more_specs,
            out_specs=[
                whole((SLOTS, WIDE)),
                pl.BlockSpec((1, 2, 1, WIDE, 128), lambda i, info: (i % 2, info[0], i // 2, 0, 0)),
            ],
        ),
        out_shape=[shape_of((SLOTS, WIDE), F32), shape_of((ZP, Y, 2, WIDE, 128), BF)],
        input_output_aliases=aliases,
        compiler_params=LIMIT,
        cost_estimate=pl.CostEstimate(flops=805 * 10**6, bytes_accessed=4 * 10**6, transcendentals=0),
    )(info, shards, w_out.reshape(ZH * X * CORE, WIDE, WIDE), scaled_t, *more)


def fold_kernel(info_ref, moved_ref, *refs):
    refs[-1][0] = jnp.sum(moved_ref[...].astype(F32), axis=0)[0].astype(BF)


def fold(half, moved, begin=None):
    more = [] if begin is None else [begin]
    return pl.pallas_call(
        fold_kernel,
        grid_spec=pltpu.PrefetchScalarGridSpec(
            num_scalar_prefetch=1,
            grid=(2,),
            in_specs=[pl.BlockSpec((ZP * Y, 1, WIDE, 128), lambda i, info: (0, i, 0, 0))]
            + [pl.BlockSpec(memory_space=pl.ANY) for _ in more],
            out_specs=pl.BlockSpec((1, WIDE, 128), lambda i, info: (info[0] * 2 + i, 0, 0)),
        ),
        out_shape=shape_of((ZQ, WIDE, 128), BF),
        input_output_aliases={2: 0} if more else {},
        compiler_params=LIMIT,
        cost_estimate=pl.CostEstimate(flops=1 * 10**6, bytes_accessed=2 * 10**6, transcendentals=0),
    )(half.astype(jnp.int32).reshape(1), moved, *more)


def over_zp_y(blocks):
    blocks = blocks.reshape(ZP * Y, 2, WIDE, 128)
    return lax.all_to_all(blocks, ("zp", "y"), 0, 0, tiled=True)


PICK = 512


def pick_kernel(row_ref, cot_ref, out_ref, col_ref, sum_ref):
    step = pl.program_id(0)

    @pl.when(step == 0)
    def _():
        sum_ref[...] = jnp.zeros_like(sum_ref)
        for a in range(SLOTS // 128):
            lanes = slice(a * 128, (a + 1) * 128)
            col_ref[lanes, :] = jnp.broadcast_to(row_ref[:, lanes], (128, 128)).T

    lane = lax.broadcasted_iota(jnp.int32, (SLOTS, 128), 1).astype(F32)
    total = sum_ref[...]
    for b in range(PICK // 128):
        token = lane + (step * PICK + b * 128).astype(F32)
        hot = jnp.where(col_ref[...] == token, 1.0, 0.0).astype(BF)
        total = total + jnp.dot(hot, cot_ref[b * 128 : (b + 1) * 128, :], preferred_element_type=F32)
    sum_ref[...] = total

    @pl.when(step == pl.num_programs(0) - 1)
    def _():
        rows = total.astype(BF)
        for a in range(X):
            out_ref[a] = rows


def pick(cotangent, live_positions):
    tokens = cotangent.shape[0]
    return pl.pallas_call(
        pick_kernel,
        grid=(tokens // PICK,),
        in_specs=[
            pl.BlockSpec((1, SLOTS), lambda i: (0, 0)),
            pl.BlockSpec((PICK, WIDE), lambda i: (i, 0)),
        ],
        out_specs=pl.BlockSpec((X, SLOTS, WIDE), lambda i: (0, 0, 0)),
        out_shape=shape_of((X, SLOTS, WIDE), BF),
        scratch_shapes=[pltpu.VMEM((SLOTS, 128), F32), pltpu.VMEM((SLOTS, WIDE), F32)],
        compiler_params=LIMIT,
        cost_estimate=pl.CostEstimate(flops=1208 * 10**6, bytes_accessed=3 * 10**6, transcendentals=0),
    )(live_positions.astype(F32), cotangent)


def packed(router):
    lead = lax.reduce_precision(router, 8, 7)
    terms = jnp.concatenate([lead, router - lead]).astype(BF).reshape(-1, WIDE)
    return jnp.pad(terms, ((0, EXTRA - terms.shape[0]), (0, 0)))


def unpacked(rows):
    terms = rows[: 2 * SLOTS // WIDE].astype(F32).reshape(2, SLOTS)
    return terms[0] + terms[1]


def per_device(cotangent, routed, counts, logits, query_rows, key_rows, routed_value_rows, w_out):
    zh, x, core = lax.axis_index("zh"), lax.axis_index("x"), lax.axis_index("core")
    dp_index = (lax.axis_index("zq") * ZP + lax.axis_index("zp")) * Y + lax.axis_index("y")
    own = jnp.arange(counts.shape[0], dtype=jnp.int32) == dp_index
    own_count = jnp.sum(jnp.where(own, counts, 0))
    positions = routed[0]
    live = jnp.arange(SLOTS, dtype=jnp.int32) < own_count
    copies = pick(cotangent[0], jnp.where(live, positions, -1)[None, :])

    sizes = range(STEP, SLOTS + 1, STEP)
    branch = jnp.maximum(own_count - 1, 0) // STEP
    other_copies, own_near = lax.switch(
        branch, [functools.partial(exchange, rows) for rows in sizes], copies
    )
    other_near = spread_x(other_copies)
    own_far = swap(own_near, "core")

    info = jnp.stack([x // 2, own_count]).astype(jnp.int32)
    attention = (
        info, query_rows[0], key_rows[0], routed_value_rows[0],
        positions[:, None], positions[None, :], logits[0][:, None],
    )
    attended, scaled_t, lse = forward(*attention)
    begun, w_grad_own = products(core, zh, own_near, w_out, scaled_t)
    begun, w_grad_own = products(1 - core, zh, own_far, w_out, scaled_t, begun, w_grad_own)

    other_near, begun, w_grad_own = lax.optimization_barrier((other_near, begun, w_grad_own))
    other_far = swap(other_near, "core")
    moved_own = over_zp_y(w_grad_own)
    begun, w_grad_other = products(core, 1 - zh, other_near, w_out, scaled_t, begun)
    grad_o, w_grad_other = products(1 - core, 1 - zh, other_far, w_out, scaled_t, begun, w_grad_other)
    moved_other = over_zp_y(w_grad_other)

    grad_q, kv, router = backward(*attention, lse, attended, grad_o)
    moved_other, _ = lax.optimization_barrier((moved_other, kv))
    blocks = fold(zh, moved_own)
    blocks = fold(1 - zh, moved_other, blocks)
    final = lax.all_to_all(blocks, "zq", 0, 0, tiled=True)
    w_grad = jnp.sum(final.astype(F32), axis=0).T.astype(BF)

    router = router[:, 0]
    half = SLOTS // 2
    kept = lax.dynamic_slice_in_dim(kv, core * half, half, 0)
    sent = lax.dynamic_slice_in_dim(kv, (1 - core) * half, half, 0)
    came = swap(jnp.concatenate([sent, packed(router)], 0), "core")
    chip = (kept.astype(F32) + came[:half].astype(F32)).astype(BF)
    router = router + unpacked(came[half:])
    pieces = spread_x(repeated(jnp.concatenate([chip, packed(router)], 0)))

    wide = pieces[:, :half].astype(F32)
    first, second = wide[0] + wide[1], wide[2] + wide[3]
    joined = jnp.concatenate(
        [first[:, :HEAD_SIZE], second[:, :HEAD_SIZE], first[:, HEAD_SIZE:], second[:, HEAD_SIZE:]], 1
    ).astype(BF)
    theirs = swap(joined, "core")
    router = sum(unpacked(pieces[s, half:]) for s in range(X))
    router = router + swap(router, "zh")
    rows = jnp.where(
        core == 0, jnp.concatenate([joined, theirs], 0), jnp.concatenate([theirs, joined], 0)
    )
    key_total, value_total = rows[:, : 2 * HEAD_SIZE], rows[:, 2 * HEAD_SIZE :]
    router_weight = jax.nn.sigmoid(logits[0])
    grad_logits = router * router_weight * (1.0 - router_weight)
    return (grad_q[None], key_total[None], value_total[None], w_grad, grad_logits[None])


def solution(mesh):
    fine = Mesh(mesh.devices.reshape(ZQ, ZP, Y, ZH, X, CORE), ("zq", "zp", "y", "zh", "x", "core"))
    dp, col = ("zq", "zp", "y"), ("x", "core")
    row_col = ("zh",) + col
    placed = (
        P(dp, None, row_col),
        P(dp, None),
        P(),
        P(dp, None),
        P(dp, None, row_col),
        P(dp, None, "zh"),
        P(dp, None, "zh"),
        P(None, row_col),
    )
    return jax.shard_map(
        per_device,
        mesh=fine,
        in_specs=placed,
        out_specs=(
            P(dp, None, row_col),
            P(dp, None, "zh"),
            P(dp, None, "zh"),
            P(dp, row_col),
            P(dp, None),
        ),
        check_vma=False,
    )
```

```python
import functools

import jax
import jax.numpy as jnp
from jax import lax
from jax.experimental import pallas as pl
from jax.experimental.pallas import tpu as pltpu
from jax.sharding import Mesh
from jax.sharding import PartitionSpec as P

HEAD_SIZE = 128
ZQ, ZP, Y, ZH, X, CORE = 4, 2, 4, 2, 4, 2
SLOTS, WIDE, HEADS = 768, 256, 2
SCALE = HEAD_SIZE ** (-0.5)
BF, F32 = jnp.bfloat16, jnp.float32
ROWS = 256
STEP = 64
HALF, EXTRA = SLOTS // 2, 16
LIMIT = pltpu.CompilerParams(vmem_limit_bytes=24 * 1024 * 1024)


def ring(n, k):
    return [(i, (i + k) % n) for i in range(n)]


def swap(value, axis):
    return lax.ppermute(value, axis, ring(2, 1))


def spread_x(copies):
    return lax.all_to_all(copies, "x", 0, 0, tiled=True)


def repeated(block):
    return jnp.broadcast_to(block[None], (X,) + block.shape)


def exchange(rows, picked, attention):
    other = swap(picked[:rows], "zh")
    near = spread_x(repeated(picked))
    other = jnp.pad(other, ((0, SLOTS - rows), (0, 0)))
    return repeated(other), near, forward(*attention)


def transposed_dot(a, b):
    return lax.dot_general(a, b, (((0,), (0,)), ((), ())), preferred_element_type=F32)


def rows_dot(a, b):
    return lax.dot_general(a, b, (((1,), (1,)), ((), ())), preferred_element_type=F32)


def column(row):
    parts = [
        jnp.broadcast_to(row[:, a : a + 128], (128, 128)).T for a in range(0, row.shape[1], 128)
    ]
    return jnp.concatenate(parts, axis=0)[:, :1]


def allowed_block(info_ref, pos_col, pos_row):
    first = pl.program_id(0) * ROWS
    shape = (ROWS, SLOTS)
    i = lax.broadcasted_iota(jnp.int32, shape, 0) + first
    j = lax.broadcasted_iota(jnp.int32, shape, 1)
    return ((j < info_ref[1]) & (pos_row <= pos_col)) | (i == j)


def forward_kernel(info_ref, q_ref, k_ref, v_ref, col_ref, row_ref, logit_ref, att_ref, scaled_ref, lse_ref):
    allowed = allowed_block(info_ref, column(col_ref[...]), row_ref[...])
    weight = 1.0 / (1.0 + jnp.exp(-column(logit_ref[...])))
    for h in range(HEADS):
        lanes = slice(h * HEAD_SIZE, (h + 1) * HEAD_SIZE)
        s = rows_dot(q_ref[:, lanes], k_ref[...]) * SCALE
        s = jnp.where(allowed, s, -1e30)
        top = jnp.max(s, axis=1, keepdims=True)
        e = jnp.exp(s - top)
        total = jnp.sum(e, axis=1, keepdims=True)
        p = (e * (1.0 / total)).astype(BF)
        att = jnp.dot(p, v_ref[...], preferred_element_type=F32).astype(BF)
        att_ref[:, lanes] = att
        scaled_ref[lanes, :] = (weight * att.astype(F32)).astype(BF).T
        lse_ref[:, h : h + 1] = top + jnp.log(total)


def backward_kernel(
    info_ref, q_ref, k_ref, v_ref, col_ref, row_ref, logit_ref, lse_ref, att_ref, go_ref,
    gq_ref, kept_ref, sent_ref, router_ref, sum_ref, terms_ref,
):
    step = pl.program_id(0)
    allowed = allowed_block(info_ref, column(col_ref[...]), row_ref[...])
    weight = 1.0 / (1.0 + jnp.exp(-column(logit_ref[...])))
    grad_o = go_ref[...]
    router = jnp.sum(grad_o * att_ref[...].astype(F32), axis=1, keepdims=True)
    router = jnp.broadcast_to(router, (ROWS, 128)).T[:1]
    router_ref[...] = router
    lead = router.astype(BF).astype(F32)
    grad_attn = (weight * grad_o).astype(BF)

    @pl.when(step == 0)
    def _():
        sum_ref[...] = jnp.zeros_like(sum_ref)
        terms_ref[...] = jnp.zeros_like(terms_ref)

    terms_ref[pl.ds(step, 1), :] = lead
    terms_ref[pl.ds(step + SLOTS // ROWS, 1), :] = router - lead
    for h in range(HEADS):
        lanes = slice(h * HEAD_SIZE, (h + 1) * HEAD_SIZE)
        q = q_ref[:, lanes]
        s = rows_dot(q, k_ref[...]) * SCALE
        p = jnp.exp(jnp.where(allowed, s - lse_ref[:, h : h + 1], -1e30))
        ga = grad_attn[:, lanes]
        gp = rows_dot(ga, v_ref[...])
        delta = jnp.sum(p * gp, axis=1, keepdims=True)
        gs = (p * (gp - delta)).astype(BF)
        gq = jnp.dot(gs, k_ref[...], preferred_element_type=F32) * SCALE
        gq_ref[:, lanes] = gq.astype(BF)
        sum_ref[:, :HEAD_SIZE] += transposed_dot(gs, q)
        sum_ref[:, HEAD_SIZE:] += transposed_dot(p.astype(BF), ga)

    @pl.when(step == pl.num_programs(0) - 1)
    def _():
        core = info_ref[2]
        for ref, side in ((kept_ref, core), (sent_ref, 1 - core)):
            rows = pl.ds(pl.multiple_of(side * HALF, HALF), HALF)
            ref[:HALF, :HEAD_SIZE] = (sum_ref[rows, :HEAD_SIZE] * SCALE).astype(BF)
            ref[:HALF, HEAD_SIZE:] = sum_ref[rows, HEAD_SIZE:].astype(BF)
        sent_ref[HALF:, :] = terms_ref[...].astype(BF)


def by_rows(width):
    return pl.BlockSpec((ROWS, width), lambda i, info: (i, 0))


def row_part():
    return pl.BlockSpec((1, ROWS), lambda i, info: (0, i))


def by_group():
    return pl.BlockSpec((SLOTS, HEAD_SIZE), lambda i, info: (0, info[0]))


def whole(shape):
    return pl.BlockSpec(shape, lambda i, info: (0,) * len(shape))


def shape_of(shape, dtype):
    return jax.ShapeDtypeStruct(shape, dtype)


def forward(info, q, k, v, pos_col, pos_row, logit_col):
    return pl.pallas_call(
        forward_kernel,
        grid_spec=pltpu.PrefetchScalarGridSpec(
            num_scalar_prefetch=1,
            grid=(SLOTS // ROWS,),
            in_specs=[by_rows(WIDE), by_group(), by_group(), row_part(), whole((1, SLOTS)), row_part()],
            out_specs=[by_rows(WIDE), pl.BlockSpec((WIDE, ROWS), lambda i, info: (0, i)), by_rows(HEADS)],
        ),
        out_shape=[shape_of((SLOTS, WIDE), BF), shape_of((WIDE, SLOTS), BF), shape_of((SLOTS, HEADS), F32)],
        compiler_params=LIMIT,
        cost_estimate=pl.CostEstimate(flops=4 * 10**9, bytes_accessed=2 * 10**6, transcendentals=1200000),
    )(info, q, k, v, pos_col, pos_row, logit_col)


def backward(info, q, k, v, pos_col, pos_row, logit_col, lse, att, grad_o):
    return pl.pallas_call(
        backward_kernel,
        grid_spec=pltpu.PrefetchScalarGridSpec(
            num_scalar_prefetch=1,
            grid=(SLOTS // ROWS,),
            in_specs=[
                by_rows(WIDE), by_group(), by_group(), row_part(), whole((1, SLOTS)), row_part(),
                by_rows(HEADS), by_rows(WIDE), by_rows(WIDE),
            ],
            out_specs=[by_rows(WIDE), whole((HALF, WIDE)), whole((HALF + EXTRA, WIDE)), row_part()],
            scratch_shapes=[pltpu.VMEM((SLOTS, WIDE), F32), pltpu.VMEM((EXTRA, WIDE), F32)],
        ),
        out_shape=[
            shape_of((SLOTS, WIDE), BF), shape_of((HALF, WIDE), BF),
            shape_of((HALF + EXTRA, WIDE), BF), shape_of((1, SLOTS), F32),
        ],
        compiler_params=LIMIT,
        cost_estimate=pl.CostEstimate(flops=7 * 10**9, bytes_accessed=4 * 10**6, transcendentals=1200000),
    )(info, q, k, v, pos_col, pos_row, logit_col, lse, att, grad_o)


def products_kernel(info_ref, near_ref, far_ref, wn_ref, wf_ref, scaled_ref, *refs):
    go_ref, wg_ref = refs[-2:]
    core = info_ref[0]
    near, far = near_ref[0], far_ref[0]
    part = jnp.dot(near, wn_ref[0], preferred_element_type=F32)
    part = part + jnp.dot(far, wf_ref[0], preferred_element_type=F32)
    first = pl.program_id(0) == 0

    @pl.when(first)
    def _():
        go_ref[...] = part + refs[0][...] if len(refs) == 3 else part

    @pl.when(jnp.logical_not(first))
    def _():
        go_ref[...] += part

    for shard, y in ((near, 2 * core), (far, 2 - 2 * core)):
        grad = jnp.dot(scaled_ref[...], shard, preferred_element_type=F32).astype(BF)
        wg_ref[0, y, 0] = grad[:, :128]
        wg_ref[0, y + 1, 0] = grad[:, 128:]


def products(core, half, near, far, w_out, scaled_t, begin=None):
    info = jnp.stack([core, half]).astype(jnp.int32)
    more = [] if begin is None else [begin]
    shard = pl.BlockSpec((1, SLOTS, WIDE), lambda i, info: (i, 0, 0))
    w_near = pl.BlockSpec((1, WIDE, WIDE), lambda i, info: (info[1] * 8 + i * 2 + info[0], 0, 0))
    w_far = pl.BlockSpec((1, WIDE, WIDE), lambda i, info: (info[1] * 8 + i * 2 + 1 - info[0], 0, 0))
    w_parts = w_out.reshape(ZH * X * CORE, WIDE, WIDE)
    return pl.pallas_call(
        products_kernel,
        grid_spec=pltpu.PrefetchScalarGridSpec(
            num_scalar_prefetch=1,
            grid=(X,),
            in_specs=[shard, shard, w_near, w_far, whole((WIDE, SLOTS))]
            + [whole((SLOTS, WIDE)) for _ in more],
            out_specs=[
                whole((SLOTS, WIDE)),
                pl.BlockSpec((1, Y, 1, WIDE, 128), lambda i, info: (i % 2, 0, i // 2, 0, 0)),
            ],
        ),
        out_shape=[shape_of((SLOTS, WIDE), F32), shape_of((ZP, Y, 2, WIDE, 128), BF)],
        compiler_params=LIMIT,
        cost_estimate=pl.CostEstimate(flops=4 * 10**9, bytes_accessed=8 * 10**6, transcendentals=0),
    )(info, near, far, w_parts, w_parts, scaled_t, *more)


def fold_kernel(info_ref, moved_ref, *refs):
    refs[-1][0] = jnp.sum(moved_ref[...].astype(F32), axis=0)[0].astype(BF)


def fold(half, moved, begin=None):
    more = [] if begin is None else [begin]
    return pl.pallas_call(
        fold_kernel,
        grid_spec=pltpu.PrefetchScalarGridSpec(
            num_scalar_prefetch=1,
            grid=(2,),
            in_specs=[pl.BlockSpec((ZP * Y, 1, WIDE, 128), lambda i, info: (0, i, 0, 0))]
            + [pl.BlockSpec(memory_space=pl.ANY) for _ in more],
            out_specs=pl.BlockSpec((1, WIDE, 128), lambda i, info: (info[0] * 2 + i, 0, 0)),
        ),
        out_shape=shape_of((ZQ, WIDE, 128), BF),
        input_output_aliases={2: 0} if more else {},
        compiler_params=LIMIT,
        cost_estimate=pl.CostEstimate(flops=1 * 10**6, bytes_accessed=2 * 10**6, transcendentals=0),
    )(half.astype(jnp.int32).reshape(1), moved, *more)


def over_zp_y(blocks):
    blocks = blocks.reshape(ZP * Y, 2, WIDE, 128)
    return lax.all_to_all(blocks, ("zp", "y"), 0, 0, tiled=True)


def packed(router):
    lead = lax.reduce_precision(router, 8, 7)
    terms = jnp.concatenate([lead, router - lead]).astype(BF).reshape(-1, WIDE)
    return jnp.pad(terms, ((0, EXTRA - terms.shape[0]), (0, 0)))


def unpacked(rows):
    terms = rows[: 2 * SLOTS // WIDE].astype(F32).reshape(2, SLOTS)
    return terms[0] + terms[1]


def per_device(cotangent, routed, counts, logits, query_rows, key_rows, routed_value_rows, w_out):
    zh, x, core = lax.axis_index("zh"), lax.axis_index("x"), lax.axis_index("core")
    dp_index = (lax.axis_index("zq") * ZP + lax.axis_index("zp")) * Y + lax.axis_index("y")
    own = jnp.arange(counts.shape[0], dtype=jnp.int32) == dp_index
    own_count = jnp.sum(jnp.where(own, counts, 0))
    positions = routed[0]
    picked = cotangent[0].at[positions].get(mode="promise_in_bounds")
    live = jnp.arange(SLOTS, dtype=jnp.int32) < own_count
    picked = jnp.where(live[:, None], picked, jnp.zeros((), BF))

    info = jnp.stack([x // 2, own_count, core]).astype(jnp.int32)
    attention = (
        info, query_rows[0], key_rows[0], routed_value_rows[0],
        routed, routed, logits,
    )
    sizes = range(STEP, SLOTS + 1, STEP)
    branch = jnp.maximum(own_count - 1, 0) // STEP
    other_copies, own_near, (attended, scaled_t, lse) = lax.switch(
        branch, [functools.partial(exchange, rows) for rows in sizes], picked, attention
    )
    other_near = spread_x(other_copies)
    own_far = swap(own_near, "core")
    begun, w_grad_own = products(core, zh, own_near, own_far, w_out, scaled_t)

    other_near, begun, w_grad_own = lax.optimization_barrier((other_near, begun, w_grad_own))
    other_far = swap(other_near, "core")
    moved_own = over_zp_y(w_grad_own)
    grad_o, w_grad_other = products(core, 1 - zh, other_near, other_far, w_out, scaled_t, begun)

    moved_own, grad_o, w_grad_other = lax.optimization_barrier((moved_own, grad_o, w_grad_other))
    moved_other = over_zp_y(w_grad_other)
    blocks = fold(zh, moved_own)
    grad_q, kept, sent, router = backward(*attention, lse, attended, grad_o)
    came = swap(sent, "core")
    chip = (kept.astype(F32) + came[:HALF].astype(F32)).astype(BF)
    chip = jnp.concatenate([chip, packed(router[0] + unpacked(came[HALF:]))], 0)

    moved_other, blocks, chip = lax.optimization_barrier((moved_other, blocks, chip))
    blocks = fold(1 - zh, moved_other, blocks)
    final = lax.all_to_all(blocks, "zq", 0, 0, tiled=True)
    w_grad = jnp.sum(final.astype(F32), axis=0).T.astype(BF)

    pieces = [chip] + [lax.ppermute(chip, "x", ring(X, k)) for k in (1, 2, 3)]
    wide = [piece[:HALF].astype(F32) for piece in pieces]
    first = sum(jnp.where((x - k) % X < 2, wide[k], 0.0) for k in range(X))
    second = sum(jnp.where((x - k) % X < 2, 0.0, wide[k]) for k in range(X))
    joined = jnp.concatenate(
        [first[:, :HEAD_SIZE], second[:, :HEAD_SIZE], first[:, HEAD_SIZE:], second[:, HEAD_SIZE:]], 1
    ).astype(BF)
    theirs = swap(joined, "core")
    router = sum(unpacked(piece[HALF:]) for piece in pieces)
    router = router + swap(router, "zh")
    rows = jnp.where(
        core == 0, jnp.concatenate([joined, theirs], 0), jnp.concatenate([theirs, joined], 0)
    )
    key_total, value_total = rows[:, : 2 * HEAD_SIZE], rows[:, 2 * HEAD_SIZE :]
    router_weight = jax.nn.sigmoid(logits[0])
    grad_logits = router * router_weight * (1.0 - router_weight)
    return (grad_q[None], key_total[None], value_total[None], w_grad, grad_logits[None])


def solution(mesh):
    fine = Mesh(mesh.devices.reshape(ZQ, ZP, Y, ZH, X, CORE), ("zq", "zp", "y", "zh", "x", "core"))
    dp, col = ("zq", "zp", "y"), ("x", "core")
    row_col = ("zh",) + col
    placed = (
        P(dp, None, row_col),
        P(dp, None),
        P(),
        P(dp, None),
        P(dp, None, row_col),
        P(dp, None, "zh"),
        P(dp, None, "zh"),
        P(None, row_col),
    )
    return jax.shard_map(
        per_device,
        mesh=fine,
        in_specs=placed,
        out_specs=(
            P(dp, None, row_col),
            P(dp, None, "zh"),
            P(dp, None, "zh"),
            P(dp, row_col),
            P(dp, None),
        ),
        check_vma=False,
    )
```

```python
import functools

import jax
import jax.numpy as jnp
from jax import lax
from jax.experimental import pallas as pl
from jax.experimental.pallas import tpu as pltpu
from jax.sharding import Mesh
from jax.sharding import PartitionSpec as P

HEAD_SIZE = 128
ZQ, ZP, Y, ZH, X, CORE = 4, 2, 4, 2, 4, 2
SLOTS, WIDE, HEADS = 768, 256, 2
SCALE = HEAD_SIZE ** (-0.5)
BF, F32 = jnp.bfloat16, jnp.float32
ROWS = 256
STEP = 64
PAD_COST = 10**6
CHUNK = 128
CHUNKS = range(0, SLOTS, CHUNK)
HALF, EXTRA = SLOTS // 2, 16
LIMIT = pltpu.CompilerParams(vmem_limit_bytes=60 * 1024 * 1024)
SMALL = pltpu.CompilerParams(vmem_limit_bytes=16 * 1024 * 1024)


def ring(n, k):
    return [(i, (i + k) % n) for i in range(n)]


def swap(value, axis):
    return lax.ppermute(value, axis, ring(2, 1))


def spread_x(copies):
    return lax.all_to_all(copies, "x", 0, 0, tiled=True)


def repeated(block):
    return jnp.broadcast_to(block[None], (X,) + block.shape)


def pad_kernel(rows_ref, out_ref):
    rows = rows_ref.shape[0]
    out_ref[:rows] = rows_ref[...]
    if rows < SLOTS:
        out_ref[rows:] = jnp.zeros((SLOTS - rows, WIDE), BF)


def padded(rows):
    return pl.pallas_call(
        pad_kernel,
        out_shape=shape_of((SLOTS, WIDE), BF),
        compiler_params=SMALL,
        cost_estimate=pl.CostEstimate(flops=PAD_COST, bytes_accessed=10**6, transcendentals=0),
    )(rows)


def exchange(rows, picked, attention):
    other = padded(swap(picked[:rows], "zh"))
    near = spread_x(repeated(picked))
    return other, near, forward(*attention)


def rows_dot(a, b):
    return lax.dot_general(a, b, (((1,), (1,)), ((), ())), preferred_element_type=F32)


def column(row):
    parts = [
        jnp.broadcast_to(row[:, a : a + 128], (128, 128)).T for a in range(0, row.shape[1], 128)
    ]
    return jnp.concatenate(parts, axis=0)[:, :1]


def key_positions(info_ref, pos_row):
    j = lax.broadcasted_iota(jnp.int32, (1, SLOTS), 1)
    return jnp.broadcast_to(column(jnp.where(j < info_ref[1], pos_row, 1 << 20)), (SLOTS, ROWS))


def allowed_block(key_ref, pos_ref, first):
    shape = (CHUNK, ROWS)
    ahead = lax.broadcasted_iota(jnp.int32, shape, 0) - lax.broadcasted_iota(jnp.int32, shape, 1)
    same = ahead == pl.program_id(0) * ROWS - first
    return (key_ref[first : first + CHUNK, :] <= pos_ref[...]) | same


def forward_kernel(
    info_ref, q_ref, k_ref, v_ref, pos_ref, row_ref, logit_ref,
    att_ref, scaled_ref, lse_ref, key_ref, vt_ref,
):
    @pl.when(pl.program_id(0) == 0)
    def _():
        key_ref[...] = key_positions(info_ref, row_ref[...])
        vt_ref[...] = v_ref[...].astype(F32).T.astype(BF)

    weight = 1.0 / (1.0 + jnp.exp(-logit_ref[...]))
    allowed = [allowed_block(key_ref, pos_ref, c) for c in CHUNKS]
    for h in range(HEADS):
        lanes = slice(h * HEAD_SIZE, (h + 1) * HEAD_SIZE)
        q = q_ref[:, lanes]
        s = [
            jnp.where(seen, rows_dot(k_ref[c : c + CHUNK, :], q) * SCALE, -1e30)
            for c, seen in zip(CHUNKS, allowed)
        ]
        top = functools.reduce(jnp.maximum, [jnp.max(t, axis=0, keepdims=True) for t in s])
        e = [jnp.exp(t - top) for t in s]
        total = sum(jnp.sum(t, axis=0, keepdims=True) for t in e)
        scale = 1.0 / total
        p = jnp.concatenate([(t * scale).astype(BF) for t in e], 0)
        att = jnp.dot(vt_ref[...], p, preferred_element_type=F32).astype(BF).astype(F32)
        att_ref[:, lanes] = att.T.astype(BF)
        scaled_ref[lanes, :] = (weight * att).astype(BF)
        lse_ref[h : h + 1, :] = top + jnp.log(total)


def backward_kernel(
    info_ref, q_ref, k_ref, v_ref, pos_ref, row_ref, logit_ref, lse_ref, att_ref, go_ref,
    gq_ref, kept_ref, sent_ref, sum_ref, terms_ref, key_ref, kt_ref,
):
    step = pl.program_id(0)

    @pl.when(step == 0)
    def _():
        sum_ref[...] = jnp.zeros_like(sum_ref)
        terms_ref[...] = jnp.zeros_like(terms_ref)
        key_ref[...] = key_positions(info_ref, row_ref[...])
        kt_ref[...] = k_ref[...].astype(F32).T.astype(BF)

    allowed = [allowed_block(key_ref, pos_ref, c) for c in CHUNKS]
    weight = 1.0 / (1.0 + jnp.exp(-column(logit_ref[...])))
    grad_o = go_ref[...]
    grad_attn = (weight * grad_o).astype(BF)
    router = jnp.sum(grad_o * att_ref[...].astype(F32), axis=1, keepdims=True)
    router = jnp.broadcast_to(router, (ROWS, 128)).T[:1]
    lead = router.astype(BF).astype(F32)
    terms_ref[pl.ds(step, 1), :] = lead
    terms_ref[pl.ds(step + SLOTS // ROWS, 1), :] = router - lead
    for h in range(HEADS):
        lanes = slice(h * HEAD_SIZE, (h + 1) * HEAD_SIZE)
        q = q_ref[:, lanes]
        ga = grad_attn[:, lanes]
        lse = lse_ref[h : h + 1, :]
        p, gp, delta = [], [], jnp.zeros((1, ROWS), F32)
        for c, seen in zip(CHUNKS, allowed):
            s = rows_dot(k_ref[c : c + CHUNK, :], q) * SCALE
            p.append(jnp.exp(jnp.where(seen, s - lse, -1e30)))
            gp.append(rows_dot(v_ref[c : c + CHUNK, :], ga))
            delta = delta + jnp.sum(p[-1] * gp[-1], axis=0, keepdims=True)
        gs = [(a * (b - delta)).astype(BF) for a, b in zip(p, gp)]
        for c, a, b in zip(CHUNKS, gs, p):
            rows = slice(c, c + CHUNK)
            sum_ref[rows, :HEAD_SIZE] += jnp.dot(a, q, preferred_element_type=F32)
            sum_ref[rows, HEAD_SIZE:] += jnp.dot(b.astype(BF), ga, preferred_element_type=F32)
        gs = jnp.concatenate(gs, 0)
        gq = jnp.dot(kt_ref[...], gs, preferred_element_type=F32) * SCALE
        gq_ref[:, lanes] = gq.T.astype(BF)

    @pl.when(step == pl.num_programs(0) - 1)
    def _():
        core = info_ref[2]
        for ref, side in ((kept_ref, core), (sent_ref, 1 - core)):
            rows = pl.ds(pl.multiple_of(side * HALF, HALF), HALF)
            ref[:HALF, :HEAD_SIZE] = (sum_ref[rows, :HEAD_SIZE] * SCALE).astype(BF)
            ref[:HALF, HEAD_SIZE:] = sum_ref[rows, HEAD_SIZE:].astype(BF)
            ref[HALF:, :] = terms_ref[...].astype(BF)


def by_rows(width):
    return pl.BlockSpec((ROWS, width), lambda i, info: (i, 0))


def row_part():
    return pl.BlockSpec((1, ROWS), lambda i, info: (0, i))


def by_heads():
    return pl.BlockSpec((HEADS, ROWS), lambda i, info: (0, i))


def by_group():
    return pl.BlockSpec((SLOTS, HEAD_SIZE), lambda i, info: (0, info[0]))


def whole(shape):
    return pl.BlockSpec(shape, lambda i, info: (0,) * len(shape))


def shape_of(shape, dtype):
    return jax.ShapeDtypeStruct(shape, dtype)


def forward(info, q, k, v, pos_col, pos_row, logit_col):
    return pl.pallas_call(
        forward_kernel,
        grid_spec=pltpu.PrefetchScalarGridSpec(
            num_scalar_prefetch=1,
            grid=(SLOTS // ROWS,),
            in_specs=[by_rows(WIDE), by_group(), by_group(), row_part(), whole((1, SLOTS)), row_part()],
            out_specs=[by_rows(WIDE), pl.BlockSpec((WIDE, ROWS), lambda i, info: (0, i)), by_heads()],
            scratch_shapes=[pltpu.VMEM((SLOTS, ROWS), jnp.int32), pltpu.VMEM((HEAD_SIZE, SLOTS), BF)],
        ),
        out_shape=[shape_of((SLOTS, WIDE), BF), shape_of((WIDE, SLOTS), BF), shape_of((HEADS, SLOTS), F32)],
        compiler_params=SMALL,
        cost_estimate=pl.CostEstimate(flops=4 * 10**9, bytes_accessed=2 * 10**6, transcendentals=1200000),
    )(info, q, k, v, pos_col, pos_row, logit_col)


def backward(info, q, k, v, pos_col, pos_row, logit_col, lse, att, grad_o):
    return pl.pallas_call(
        backward_kernel,
        grid_spec=pltpu.PrefetchScalarGridSpec(
            num_scalar_prefetch=1,
            grid=(SLOTS // ROWS,),
            in_specs=[
                by_rows(WIDE), by_group(), by_group(), row_part(), whole((1, SLOTS)), row_part(),
                by_heads(), by_rows(WIDE), by_rows(WIDE),
            ],
            out_specs=[by_rows(WIDE), whole((HALF + EXTRA, WIDE)), whole((HALF + EXTRA, WIDE))],
            scratch_shapes=[
                pltpu.VMEM((SLOTS, WIDE), F32), pltpu.VMEM((EXTRA, WIDE), F32),
                pltpu.VMEM((SLOTS, ROWS), jnp.int32), pltpu.VMEM((HEAD_SIZE, SLOTS), BF),
            ],
        ),
        out_shape=[
            shape_of((SLOTS, WIDE), BF), shape_of((HALF + EXTRA, WIDE), BF),
            shape_of((HALF + EXTRA, WIDE), BF),
        ],
        compiler_params=LIMIT,
        cost_estimate=pl.CostEstimate(flops=7 * 10**9, bytes_accessed=4 * 10**6, transcendentals=1200000),
    )(info, q, k, v, pos_col, pos_row, logit_col, lse, att, grad_o)


def products_kernel(info_ref, near_ref, far_ref, wn_ref, wf_ref, scaled_ref, *refs):
    go_ref, wg_ref = refs[-2:]
    core = info_ref[0]
    near, far = near_ref[0], far_ref[0]
    first = pl.program_id(0) == 0

    @pl.when(first)
    def _():
        go_ref[...] = refs[0][...] if len(refs) == 3 else jnp.zeros_like(go_ref)

    w = jnp.concatenate([wn_ref[0], wf_ref[0]], 0)
    for r in range(0, SLOTS, 128):
        rows = slice(r, r + 128)
        both = jnp.concatenate([near_ref[0, rows], far_ref[0, rows]], 1)
        go_ref[rows] += jnp.dot(both, w, preferred_element_type=F32)

    for shard, y in ((near, 2 * core), (far, 2 - 2 * core)):
        grad = jnp.dot(scaled_ref[...], shard, preferred_element_type=F32).astype(BF)
        wg_ref[0, y, 0] = grad[:, :128]
        wg_ref[0, y + 1, 0] = grad[:, 128:]


def products(core, half, base, turn, near, far, w_out, scaled_t, begin=None):
    info = jnp.stack([core, half, base, turn]).astype(jnp.int32)
    more = [] if begin is None else [begin]
    shard = pl.BlockSpec((1, SLOTS, WIDE), lambda i, info: (i, 0, 0))
    at = lambda i, info: (info[2] + info[3] * i) % X
    w_near = pl.BlockSpec((1, WIDE, WIDE), lambda i, info: (info[1] * 8 + at(i, info) * 2 + info[0], 0, 0))
    w_far = pl.BlockSpec((1, WIDE, WIDE), lambda i, info: (info[1] * 8 + at(i, info) * 2 + 1 - info[0], 0, 0))
    w_parts = w_out.reshape(ZH * X * CORE, WIDE, WIDE)
    return pl.pallas_call(
        products_kernel,
        grid_spec=pltpu.PrefetchScalarGridSpec(
            num_scalar_prefetch=1,
            grid=(X,),
            in_specs=[shard, shard, w_near, w_far, whole((WIDE, SLOTS))]
            + [whole((SLOTS, WIDE)) for _ in more],
            out_specs=[
                whole((SLOTS, WIDE)),
                pl.BlockSpec((1, Y, 1, WIDE, 128), lambda i, info: (at(i, info) % 2, 0, at(i, info) // 2, 0, 0)),
            ],
        ),
        out_shape=[shape_of((SLOTS, WIDE), F32), shape_of((ZP, Y, 2, WIDE, 128), BF)],
        compiler_params=LIMIT,
        cost_estimate=pl.CostEstimate(flops=2 * 10**10, bytes_accessed=8 * 10**6, transcendentals=0),
    )(info, near, far, w_parts, w_parts, scaled_t, *more)


def fold_kernel(info_ref, moved_ref, *refs):
    refs[-1][0] = jnp.sum(moved_ref[...].astype(F32), axis=0)[0].astype(BF)


def fold(half, moved, begin=None):
    more = [] if begin is None else [begin]
    return pl.pallas_call(
        fold_kernel,
        grid_spec=pltpu.PrefetchScalarGridSpec(
            num_scalar_prefetch=1,
            grid=(2,),
            in_specs=[pl.BlockSpec((ZP * Y, 1, WIDE, 128), lambda i, info: (0, i, 0, 0))]
            + [pl.BlockSpec(memory_space=pl.ANY) for _ in more],
            out_specs=pl.BlockSpec((1, WIDE, 128), lambda i, info: (info[0] * 2 + i, 0, 0)),
        ),
        out_shape=shape_of((ZQ, WIDE, 128), BF),
        input_output_aliases={2: 0} if more else {},
        compiler_params=SMALL,
        cost_estimate=pl.CostEstimate(flops=1 * 10**6, bytes_accessed=2 * 10**6, transcendentals=0),
    )(half.astype(jnp.int32).reshape(1), moved, *more)


def over_zp_y(blocks):
    blocks = blocks.reshape(ZP * Y, 2, WIDE, 128)
    return lax.all_to_all(blocks, ("zp", "y"), 0, 0, tiled=True)


def per_device(cotangent, routed, counts, logits, query_rows, key_rows, routed_value_rows, w_out):
    zh, x, core = lax.axis_index("zh"), lax.axis_index("x"), lax.axis_index("core")
    dp_index = (lax.axis_index("zq") * ZP + lax.axis_index("zp")) * Y + lax.axis_index("y")
    own = jnp.arange(counts.shape[0], dtype=jnp.int32) == dp_index
    own_count = jnp.sum(jnp.where(own, counts, 0))
    positions = routed[0]
    picked = cotangent[0].at[positions].get(mode="promise_in_bounds", wrap_negative_indices=False)
    live = jnp.arange(SLOTS, dtype=jnp.int32) < own_count
    picked = lax.optimization_barrier(jnp.where(live[:, None], picked, jnp.zeros((), BF)))

    info = jnp.stack([x // 2, own_count, core]).astype(jnp.int32)
    attention = (
        info, query_rows[0], key_rows[0], routed_value_rows[0],
        routed, routed, logits,
    )
    sizes = range(STEP, SLOTS + 1, STEP)
    branch = jnp.maximum(own_count - 1, 0) // STEP
    other, own_near, (attended, scaled_t, lse) = lax.switch(
        branch, [functools.partial(exchange, rows) for rows in sizes], picked, attention
    )
    other_near = jnp.stack([other] + [lax.ppermute(other, "x", ring(X, k)) for k in range(1, X)])
    own_far = swap(own_near, "core")
    begun, w_grad_own = products(core, zh, 0, 1, own_near, own_far, w_out, scaled_t)

    other_near, begun = lax.optimization_barrier((other_near, begun))
    other_far = swap(other_near, "core")
    moved_own = over_zp_y(w_grad_own)
    grad_o, w_grad_other = products(core, 1 - zh, x, 3, other_near, other_far, w_out, scaled_t, begun)

    moved_own, grad_o, w_grad_other = lax.optimization_barrier((moved_own, grad_o, w_grad_other))
    moved_other = over_zp_y(w_grad_other)
    blocks = fold(zh, moved_own)
    grad_q, kept, sent = backward(*attention, lse, attended, grad_o)
    came = swap(sent, "core")
    chip = (kept.astype(F32) + came.astype(F32)).astype(BF)

    moved_other, blocks, chip = lax.optimization_barrier((moved_other, blocks, chip))
    pair = lax.ppermute(chip, "x", [(0, 1), (1, 0), (2, 3), (3, 2)])
    blocks = fold(1 - zh, moved_other, blocks)
    pair, blocks = lax.optimization_barrier((pair, blocks))
    final = lax.all_to_all(blocks, "zq", 0, 0, tiled=True)
    w_grad = jnp.sum(final.astype(F32), axis=0).T.astype(BF)

    group = (chip.astype(F32) + pair.astype(F32)).astype(BF)
    apart = lax.ppermute(group, "x", [(0, 3), (3, 0), (1, 2), (2, 1)])
    router = group[HALF:].astype(F32) + apart[HALF:].astype(F32)
    router = (router[: SLOTS // WIDE] + router[SLOTS // WIDE : 2 * SLOTS // WIDE]).reshape(SLOTS)
    first = jnp.where(x < 2, group, apart)[:HALF]
    second = jnp.where(x < 2, apart, group)[:HALF]
    joined = jnp.concatenate(
        [first[:, :HEAD_SIZE], second[:, :HEAD_SIZE], first[:, HEAD_SIZE:], second[:, HEAD_SIZE:]], 1
    )
    theirs = swap(joined, "core")
    router = router + swap(router, "zh")
    rows = jnp.where(
        core == 0, jnp.concatenate([joined, theirs], 0), jnp.concatenate([theirs, joined], 0)
    )
    key_total, value_total = rows[:, : 2 * HEAD_SIZE], rows[:, 2 * HEAD_SIZE :]
    router_weight = jax.nn.sigmoid(logits[0])
    grad_logits = router * router_weight * (1.0 - router_weight)
    return (grad_q[None], key_total[None], value_total[None], w_grad, grad_logits[None])


def solution(mesh):
    fine = Mesh(mesh.devices.reshape(ZQ, ZP, Y, ZH, X, CORE), ("zq", "zp", "y", "zh", "x", "core"))
    dp, col = ("zq", "zp", "y"), ("x", "core")
    row_col = ("zh",) + col
    placed = (
        P(dp, None, row_col),
        P(dp, None),
        P(),
        P(dp, None),
        P(dp, None, row_col),
        P(dp, None, "zh"),
        P(dp, None, "zh"),
        P(None, row_col),
    )
    return jax.shard_map(
        per_device,
        mesh=fine,
        in_specs=placed,
        out_specs=(
            P(dp, None, row_col),
            P(dp, None, "zh"),
            P(dp, None, "zh"),
            P(dp, row_col),
            P(dp, None),
        ),
        check_vma=False,
    )
```

```python
import functools

import jax
import jax.numpy as jnp
from jax import lax
from jax.experimental import pallas as pl
from jax.experimental.pallas import tpu as pltpu
from jax.sharding import Mesh
from jax.sharding import PartitionSpec as P

HEAD_SIZE = 128
ZQ, ZP, Y, ZH, X, CORE = 4, 2, 4, 2, 4, 2
SLOTS, WIDE, HEADS = 768, 256, 2
SCALE = HEAD_SIZE ** (-0.5)
BF, F32 = jnp.bfloat16, jnp.float32
ROWS = 256
STEP = 64
PAD_COST = 10**6
CHUNK = 128
CHUNKS = range(0, SLOTS, CHUNK)
HALF, EXTRA = SLOTS // 2, 16
LIMIT = pltpu.CompilerParams(vmem_limit_bytes=60 * 1024 * 1024)
SMALL = pltpu.CompilerParams(vmem_limit_bytes=16 * 1024 * 1024)


def ring(n, k):
    return [(i, (i + k) % n) for i in range(n)]


def swap(value, axis):
    return lax.ppermute(value, axis, ring(2, 1))


def spread_x(copies):
    return lax.all_to_all(copies, "x", 0, 0, tiled=True)


def repeated(block):
    return jnp.broadcast_to(block[None], (X,) + block.shape)


def pad_kernel(rows_ref, out_ref):
    rows = rows_ref.shape[0]
    out_ref[:rows] = rows_ref[...]
    if rows < SLOTS:
        out_ref[rows:] = jnp.zeros((SLOTS - rows, WIDE), BF)


def padded(rows):
    return pl.pallas_call(
        pad_kernel,
        out_shape=shape_of((SLOTS, WIDE), BF),
        compiler_params=SMALL,
        cost_estimate=pl.CostEstimate(flops=PAD_COST, bytes_accessed=10**6, transcendentals=0),
    )(rows)


def exchange(rows, picked, scalars, attention):
    other = padded(swap(picked[:rows], "zh"))
    near = spread_x(repeated(picked))
    info = jnp.stack(scalars).astype(jnp.int32)
    return other, near, info, forward(info, *attention)


def rows_dot(a, b):
    return lax.dot_general(a, b, (((1,), (1,)), ((), ())), preferred_element_type=F32)


def column(row):
    parts = [
        jnp.broadcast_to(row[:, a : a + 128], (128, 128)).T for a in range(0, row.shape[1], 128)
    ]
    return jnp.concatenate(parts, axis=0)[:, :1]


def key_positions(info_ref, pos_row):
    j = lax.broadcasted_iota(jnp.int32, (1, SLOTS), 1)
    return jnp.broadcast_to(column(jnp.where(j < info_ref[1], pos_row, 1 << 20)), (SLOTS, ROWS))


def allowed_block(key_ref, pos_ref, first):
    shape = (CHUNK, ROWS)
    ahead = lax.broadcasted_iota(jnp.int32, shape, 0) - lax.broadcasted_iota(jnp.int32, shape, 1)
    same = ahead == pl.program_id(0) * ROWS - first
    return (key_ref[first : first + CHUNK, :] <= pos_ref[...]) | same


def forward_kernel(
    info_ref, q_ref, k_ref, v_ref, pos_ref, row_ref, logit_ref,
    att_ref, scaled_ref, lse_ref, key_ref, vt_ref,
):
    @pl.when(pl.program_id(0) == 0)
    def _():
        key_ref[...] = key_positions(info_ref, row_ref[...])
        vt_ref[...] = v_ref[...].astype(F32).T.astype(BF)

    weight = 1.0 / (1.0 + jnp.exp(-logit_ref[...]))
    allowed = [allowed_block(key_ref, pos_ref, c) for c in CHUNKS]
    for h in range(HEADS):
        lanes = slice(h * HEAD_SIZE, (h + 1) * HEAD_SIZE)
        q = q_ref[:, lanes]
        s = [
            jnp.where(seen, rows_dot(k_ref[c : c + CHUNK, :], q) * SCALE, -1e30)
            for c, seen in zip(CHUNKS, allowed)
        ]
        top = functools.reduce(jnp.maximum, [jnp.max(t, axis=0, keepdims=True) for t in s])
        e = [jnp.exp(t - top) for t in s]
        total = sum(jnp.sum(t, axis=0, keepdims=True) for t in e)
        scale = 1.0 / total
        p = jnp.concatenate([(t * scale).astype(BF) for t in e], 0)
        att = jnp.dot(vt_ref[...], p, preferred_element_type=F32).astype(BF).astype(F32)
        att_ref[:, lanes] = att.T.astype(BF)
        scaled_ref[lanes, :] = (weight * att).astype(BF)
        lse_ref[h : h + 1, :] = top + jnp.log(total)


def backward_kernel(
    info_ref, q_ref, k_ref, v_ref, pos_ref, row_ref, logit_ref, lse_ref, att_ref, go_ref,
    gq_ref, kept_ref, sent_ref, sum_ref, terms_ref, key_ref, kt_ref,
):
    step = pl.program_id(0)

    @pl.when(step == 0)
    def _():
        sum_ref[...] = jnp.zeros_like(sum_ref)
        terms_ref[...] = jnp.zeros_like(terms_ref)
        key_ref[...] = key_positions(info_ref, row_ref[...])
        kt_ref[...] = k_ref[...].astype(F32).T.astype(BF)

    allowed = [allowed_block(key_ref, pos_ref, c) for c in CHUNKS]
    weight = 1.0 / (1.0 + jnp.exp(-column(logit_ref[...])))
    grad_o = go_ref[...]
    grad_attn = (weight * grad_o).astype(BF)
    router = jnp.sum(grad_o * att_ref[...].astype(F32), axis=1, keepdims=True)
    router = jnp.broadcast_to(router, (ROWS, 128)).T[:1]
    lead = router.astype(BF).astype(F32)
    terms_ref[pl.ds(step, 1), :] = lead
    terms_ref[pl.ds(step + SLOTS // ROWS, 1), :] = router - lead
    for h in range(HEADS):
        lanes = slice(h * HEAD_SIZE, (h + 1) * HEAD_SIZE)
        q = q_ref[:, lanes]
        ga = grad_attn[:, lanes]
        lse = lse_ref[h : h + 1, :]
        p, gp, delta = [], [], jnp.zeros((1, ROWS), F32)
        for c, seen in zip(CHUNKS, allowed):
            s = rows_dot(k_ref[c : c + CHUNK, :], q) * SCALE
            p.append(jnp.exp(jnp.where(seen, s - lse, -1e30)))
            gp.append(rows_dot(v_ref[c : c + CHUNK, :], ga))
            delta = delta + jnp.sum(p[-1] * gp[-1], axis=0, keepdims=True)
        gs = [(a * (b - delta)).astype(BF) for a, b in zip(p, gp)]
        for c, a, b in zip(CHUNKS, gs, p):
            rows = slice(c, c + CHUNK)
            sum_ref[rows, :HEAD_SIZE] += jnp.dot(a, q, preferred_element_type=F32)
            sum_ref[rows, HEAD_SIZE:] += jnp.dot(b.astype(BF), ga, preferred_element_type=F32)
        gs = jnp.concatenate(gs, 0)
        gq = jnp.dot(kt_ref[...], gs, preferred_element_type=F32) * SCALE
        gq_ref[:, lanes] = gq.T.astype(BF)

    @pl.when(step == pl.num_programs(0) - 1)
    def _():
        core = info_ref[2]
        for ref, side in ((kept_ref, core), (sent_ref, 1 - core)):
            rows = pl.ds(pl.multiple_of(side * HALF, HALF), HALF)
            ref[:HALF, :HEAD_SIZE] = (sum_ref[rows, :HEAD_SIZE] * SCALE).astype(BF)
            ref[:HALF, HEAD_SIZE:] = sum_ref[rows, HEAD_SIZE:].astype(BF)
            ref[HALF:, :] = terms_ref[...].astype(BF)


def by_rows(width):
    return pl.BlockSpec((ROWS, width), lambda i, info: (i, 0))


def row_part():
    return pl.BlockSpec((1, ROWS), lambda i, info: (0, i))


def by_heads():
    return pl.BlockSpec((HEADS, ROWS), lambda i, info: (0, i))


def by_group():
    return pl.BlockSpec((SLOTS, HEAD_SIZE), lambda i, info: (0, info[0]))


def whole(shape):
    return pl.BlockSpec(shape, lambda i, info: (0,) * len(shape))


def shape_of(shape, dtype):
    return jax.ShapeDtypeStruct(shape, dtype)


def forward(info, q, k, v, pos_col, pos_row, logit_col):
    return pl.pallas_call(
        forward_kernel,
        grid_spec=pltpu.PrefetchScalarGridSpec(
            num_scalar_prefetch=1,
            grid=(SLOTS // ROWS,),
            in_specs=[by_rows(WIDE), by_group(), by_group(), row_part(), whole((1, SLOTS)), row_part()],
            out_specs=[by_rows(WIDE), pl.BlockSpec((WIDE, ROWS), lambda i, info: (0, i)), by_heads()],
            scratch_shapes=[pltpu.VMEM((SLOTS, ROWS), jnp.int32), pltpu.VMEM((HEAD_SIZE, SLOTS), BF)],
        ),
        out_shape=[shape_of((SLOTS, WIDE), BF), shape_of((WIDE, SLOTS), BF), shape_of((HEADS, SLOTS), F32)],
        compiler_params=SMALL,
        cost_estimate=pl.CostEstimate(flops=4 * 10**9, bytes_accessed=2 * 10**6, transcendentals=1200000),
    )(info, q, k, v, pos_col, pos_row, logit_col)


def backward(info, q, k, v, pos_col, pos_row, logit_col, lse, att, grad_o):
    return pl.pallas_call(
        backward_kernel,
        grid_spec=pltpu.PrefetchScalarGridSpec(
            num_scalar_prefetch=1,
            grid=(SLOTS // ROWS,),
            in_specs=[
                by_rows(WIDE), by_group(), by_group(), row_part(), whole((1, SLOTS)), row_part(),
                by_heads(), by_rows(WIDE), by_rows(WIDE),
            ],
            out_specs=[by_rows(WIDE), whole((HALF + EXTRA, WIDE)), whole((HALF + EXTRA, WIDE))],
            scratch_shapes=[
                pltpu.VMEM((SLOTS, WIDE), F32), pltpu.VMEM((EXTRA, WIDE), F32),
                pltpu.VMEM((SLOTS, ROWS), jnp.int32), pltpu.VMEM((HEAD_SIZE, SLOTS), BF),
            ],
        ),
        out_shape=[
            shape_of((SLOTS, WIDE), BF), shape_of((HALF + EXTRA, WIDE), BF),
            shape_of((HALF + EXTRA, WIDE), BF),
        ],
        compiler_params=LIMIT,
        cost_estimate=pl.CostEstimate(flops=7 * 10**9, bytes_accessed=4 * 10**6, transcendentals=1200000),
    )(info, q, k, v, pos_col, pos_row, logit_col, lse, att, grad_o)


def products_kernel(info_ref, near_ref, far_ref, w_ref, scaled_ref, *refs):
    go_ref, wg_ref = refs[-2:]
    core = info_ref[0]
    entry = [(info_ref[2] + info_ref[3] * s) % X for s in range(X)]
    w = [jnp.concatenate([w_ref[2 * s + core], w_ref[2 * s + 1 - core]], 0) for s in range(X)]
    for r in range(0, SLOTS, ROWS):
        rows = slice(r, r + ROWS)
        total = refs[0][rows] if len(refs) == 3 else jnp.zeros((ROWS, WIDE), F32)
        for s in range(X):
            both = jnp.concatenate([near_ref[entry[s], rows], far_ref[entry[s], rows]], 1)
            total = total + jnp.dot(both, w[s], preferred_element_type=F32)
        go_ref[rows] = total
    for s in range(X):
        for ref, y in ((near_ref, 2 * core), (far_ref, 2 - 2 * core)):
            grad = jnp.dot(scaled_ref[...], ref[entry[s]], preferred_element_type=F32).astype(BF)
            wg_ref[s % 2, y, s // 2] = grad[:, :128]
            wg_ref[s % 2, y + 1, s // 2] = grad[:, 128:]


def products(core, half, base, turn, near, far, w_out, scaled_t, begin=None):
    info = jnp.stack([core, half, base, turn]).astype(jnp.int32)
    more = [] if begin is None else [begin]
    shards = whole((X, SLOTS, WIDE))
    return pl.pallas_call(
        products_kernel,
        grid_spec=pltpu.PrefetchScalarGridSpec(
            num_scalar_prefetch=1,
            grid=(1,),
            in_specs=[
                shards, shards,
                pl.BlockSpec((X * CORE, WIDE, WIDE), lambda i, info: (info[1], 0, 0)),
                whole((WIDE, SLOTS)),
            ]
            + [whole((SLOTS, WIDE)) for _ in more],
            out_specs=[whole((SLOTS, WIDE)), whole((ZP, Y, 2, WIDE, 128))],
        ),
        out_shape=[shape_of((SLOTS, WIDE), F32), shape_of((ZP, Y, 2, WIDE, 128), BF)],
        compiler_params=LIMIT,
        cost_estimate=pl.CostEstimate(flops=2 * 10**10, bytes_accessed=8 * 10**6, transcendentals=0),
    )(info, near, far, w_out.reshape(ZH * X * CORE, WIDE, WIDE), scaled_t, *more)


def fold_kernel(info_ref, moved_ref, *refs):
    refs[-1][0] = jnp.sum(moved_ref[...].astype(F32), axis=0)[0].astype(BF)


def fold(half, moved, begin=None):
    more = [] if begin is None else [begin]
    return pl.pallas_call(
        fold_kernel,
        grid_spec=pltpu.PrefetchScalarGridSpec(
            num_scalar_prefetch=1,
            grid=(2,),
            in_specs=[pl.BlockSpec((ZP * Y, 1, WIDE, 128), lambda i, info: (0, i, 0, 0))]
            + [pl.BlockSpec(memory_space=pl.ANY) for _ in more],
            out_specs=pl.BlockSpec((1, WIDE, 128), lambda i, info: (info[0] * 2 + i, 0, 0)),
        ),
        out_shape=shape_of((ZQ, WIDE, 128), BF),
        input_output_aliases={2: 0} if more else {},
        compiler_params=SMALL,
        cost_estimate=pl.CostEstimate(flops=1 * 10**6, bytes_accessed=2 * 10**6, transcendentals=0),
    )(half.astype(jnp.int32).reshape(1), moved, *more)


def logits_kernel(router_ref, other_ref, logit_ref, out_ref):
    weight = 1.0 / (1.0 + jnp.exp(-logit_ref[...]))
    out_ref[...] = (router_ref[...] + other_ref[...]) * weight * (1.0 - weight)


def logits_gradient(router, other, logits):
    return pl.pallas_call(
        logits_kernel,
        out_shape=shape_of((1, SLOTS), F32),
        compiler_params=SMALL,
        cost_estimate=pl.CostEstimate(flops=2 * 10**10, bytes_accessed=10**4, transcendentals=0),
    )(router, other, logits)


def over_zp_y(blocks):
    blocks = blocks.reshape(ZP * Y, 2, WIDE, 128)
    return lax.all_to_all(blocks, ("zp", "y"), 0, 0, tiled=True)


def per_device(cotangent, routed, counts, logits, query_rows, key_rows, routed_value_rows, w_out):
    zh, x, core = lax.axis_index("zh"), lax.axis_index("x"), lax.axis_index("core")
    dp_index = (lax.axis_index("zq") * ZP + lax.axis_index("zp")) * Y + lax.axis_index("y")
    own = jnp.arange(counts.shape[0], dtype=jnp.int32) == dp_index
    own_count = jnp.sum(jnp.where(own, counts, 0))
    positions = routed[0]
    picked = cotangent[0].at[positions].get(mode="promise_in_bounds", wrap_negative_indices=False)
    live = jnp.arange(SLOTS, dtype=jnp.int32) < own_count
    picked = lax.optimization_barrier(jnp.where(live[:, None], picked, jnp.zeros((), BF)))

    attention = (
        query_rows[0], key_rows[0], routed_value_rows[0],
        routed, routed, logits,
    )
    sizes = range(STEP, SLOTS + 1, STEP)
    branch = jnp.maximum(own_count - 1, 0) // STEP
    other, own_near, info, (attended, scaled_t, lse) = lax.switch(
        branch, [functools.partial(exchange, rows) for rows in sizes], picked, (x // 2, own_count, core), attention
    )
    other_near = jnp.stack([other] + [lax.ppermute(other, "x", ring(X, k)) for k in range(1, X)])
    own_far = swap(own_near, "core")
    begun, w_grad_own = products(core, zh, 0, 1, own_near, own_far, w_out, scaled_t)

    other_near, begun = lax.optimization_barrier((other_near, begun))
    other_far = swap(other_near, "core")
    moved_own = over_zp_y(w_grad_own)
    grad_o, w_grad_other = products(core, 1 - zh, x, 3, other_near, other_far, w_out, scaled_t, begun)

    moved_own, grad_o, w_grad_other = lax.optimization_barrier((moved_own, grad_o, w_grad_other))
    moved_other = over_zp_y(w_grad_other)
    blocks = fold(zh, moved_own)
    grad_q, kept, sent = backward(info, *attention, lse, attended, grad_o)
    came = swap(sent, "core")
    chip = (kept.astype(F32) + came.astype(F32)).astype(BF)

    moved_other, blocks, chip = lax.optimization_barrier((moved_other, blocks, chip))
    pair = lax.ppermute(chip, "x", [(0, 1), (1, 0), (2, 3), (3, 2)])
    blocks = fold(1 - zh, moved_other, blocks)
    pair, blocks = lax.optimization_barrier((pair, blocks))
    final = lax.all_to_all(blocks, "zq", 0, 0, tiled=True)
    w_grad = jnp.sum(final.astype(F32), axis=0).T.astype(BF)

    group = (chip.astype(F32) + pair.astype(F32)).astype(BF)
    apart = lax.ppermute(group, "x", [(0, 3), (3, 0), (1, 2), (2, 1)])
    router = group[HALF:].astype(F32) + apart[HALF:].astype(F32)
    router = (router[: SLOTS // WIDE] + router[SLOTS // WIDE : 2 * SLOTS // WIDE]).reshape(1, SLOTS)
    first = jnp.where(x < 2, group, apart)[:HALF]
    second = jnp.where(x < 2, apart, group)[:HALF]
    joined = jnp.concatenate(
        [first[:, :HEAD_SIZE], second[:, :HEAD_SIZE], first[:, HEAD_SIZE:], second[:, HEAD_SIZE:]], 1
    )
    theirs = swap(joined, "core")
    grad_logits = logits_gradient(router, swap(router, "zh"), logits)
    rows = jnp.where(
        core == 0, jnp.concatenate([joined, theirs], 0), jnp.concatenate([theirs, joined], 0)
    )
    key_total, value_total = rows[:, : 2 * HEAD_SIZE], rows[:, 2 * HEAD_SIZE :]
    return (grad_q[None], key_total[None], value_total[None], w_grad, grad_logits)


def solution(mesh):
    fine = Mesh(mesh.devices.reshape(ZQ, ZP, Y, ZH, X, CORE), ("zq", "zp", "y", "zh", "x", "core"))
    dp, col = ("zq", "zp", "y"), ("x", "core")
    row_col = ("zh",) + col
    placed = (
        P(dp, None, row_col),
        P(dp, None),
        P(),
        P(dp, None),
        P(dp, None, row_col),
        P(dp, None, "zh"),
        P(dp, None, "zh"),
        P(None, row_col),
    )
    return jax.shard_map(
        per_device,
        mesh=fine,
        in_specs=placed,
        out_specs=(
            P(dp, None, row_col),
            P(dp, None, "zh"),
            P(dp, None, "zh"),
            P(dp, row_col),
            P(dp, None),
        ),
        check_vma=False,
    )
```

```python
import functools

import jax
import jax.numpy as jnp
from jax import lax
from jax.experimental import pallas as pl
from jax.experimental.pallas import tpu as pltpu
from jax.sharding import Mesh
from jax.sharding import PartitionSpec as P

HEAD_SIZE = 128
ZQ, ZP, Y, ZH, X, CORE = 4, 2, 4, 2, 4, 2
SLOTS, WIDE, HEADS = 768, 256, 2
SCALE = HEAD_SIZE ** (-0.5)
BF, F32 = jnp.bfloat16, jnp.float32
ROWS = 256
STEP = 64
PAD_COST = 10**6
CHUNK = 128
CHUNKS = range(0, SLOTS, CHUNK)
HALF, EXTRA = SLOTS // 2, 16
LIMIT = pltpu.CompilerParams(vmem_limit_bytes=60 * 1024 * 1024)
SMALL = pltpu.CompilerParams(vmem_limit_bytes=16 * 1024 * 1024)


def ring(n, k):
    return [(i, (i + k) % n) for i in range(n)]


def swap(value, axis):
    return lax.ppermute(value, axis, ring(2, 1))


def spread_x(copies):
    return lax.all_to_all(copies, "x", 0, 0, tiled=True)


def repeated(block):
    return jnp.broadcast_to(block[None], (X,) + block.shape)


def pad_kernel(rows_ref, out_ref):
    rows = rows_ref.shape[0]
    out_ref[:rows] = rows_ref[...]
    if rows < SLOTS:
        out_ref[rows:] = jnp.zeros((SLOTS - rows, WIDE), BF)


def padded(rows):
    return pl.pallas_call(
        pad_kernel,
        out_shape=shape_of((SLOTS, WIDE), BF),
        compiler_params=SMALL,
        cost_estimate=pl.CostEstimate(flops=PAD_COST, bytes_accessed=10**6, transcendentals=0),
    )(rows)


def exchange(rows, picked, scalars, attention):
    other = padded(swap(picked[:rows], "zh"))
    near = spread_x(repeated(picked))
    info = jnp.stack(scalars).astype(jnp.int32)
    return other, near, info, forward(info, *attention)


def rows_dot(a, b):
    return lax.dot_general(a, b, (((1,), (1,)), ((), ())), preferred_element_type=F32)


def column(row):
    parts = [
        jnp.broadcast_to(row[:, a : a + 128], (128, 128)).T for a in range(0, row.shape[1], 128)
    ]
    return jnp.concatenate(parts, axis=0)[:, :1]


def key_positions(info_ref, pos_row):
    j = lax.broadcasted_iota(jnp.int32, (1, SLOTS), 1)
    return jnp.broadcast_to(column(jnp.where(j < info_ref[1], pos_row, 1 << 20)), (SLOTS, ROWS))


def allowed_block(key_ref, pos_ref, first):
    shape = (CHUNK, ROWS)
    ahead = lax.broadcasted_iota(jnp.int32, shape, 0) - lax.broadcasted_iota(jnp.int32, shape, 1)
    same = ahead == pl.program_id(0) * ROWS - first
    return (key_ref[first : first + CHUNK, :] <= pos_ref[...]) | same


def forward_kernel(
    info_ref, q_ref, k_ref, v_ref, pos_ref, row_ref, logit_ref,
    att_ref, scaled_ref, lse_ref, key_ref, vt_ref,
):
    @pl.when(pl.program_id(0) == 0)
    def _():
        key_ref[...] = key_positions(info_ref, row_ref[...])
        vt_ref[...] = v_ref[...].astype(F32).T.astype(BF)

    weight = 1.0 / (1.0 + jnp.exp(-logit_ref[...]))
    slot = lax.broadcasted_iota(jnp.int32, (1, ROWS), 1) + pl.program_id(0) * ROWS
    weight = jnp.where(slot < info_ref[1], weight, 0.0)
    allowed = [allowed_block(key_ref, pos_ref, c) for c in CHUNKS]
    for h in range(HEADS):
        lanes = slice(h * HEAD_SIZE, (h + 1) * HEAD_SIZE)
        q = q_ref[:, lanes]
        s = [
            jnp.where(seen, rows_dot(k_ref[c : c + CHUNK, :], q) * SCALE, -1e30)
            for c, seen in zip(CHUNKS, allowed)
        ]
        top = functools.reduce(jnp.maximum, [jnp.max(t, axis=0, keepdims=True) for t in s])
        e = [jnp.exp(t - top) for t in s]
        total = sum(jnp.sum(t, axis=0, keepdims=True) for t in e)
        scale = 1.0 / total
        p = jnp.concatenate([(t * scale).astype(BF) for t in e], 0)
        att = jnp.dot(vt_ref[...], p, preferred_element_type=F32).astype(BF).astype(F32)
        att_ref[:, lanes] = att.T.astype(BF)
        scaled_ref[lanes, :] = (weight * att).astype(BF)
        lse_ref[h : h + 1, :] = top + jnp.log(total)


def backward_kernel(
    info_ref, q_ref, k_ref, v_ref, pos_ref, row_ref, logit_ref, lse_ref, att_ref, go_ref,
    gq_ref, kept_ref, sent_ref, sum_ref, terms_ref, key_ref, kt_ref,
):
    step = pl.program_id(0)

    @pl.when(step == 0)
    def _():
        sum_ref[...] = jnp.zeros_like(sum_ref)
        terms_ref[...] = jnp.zeros_like(terms_ref)
        key_ref[...] = key_positions(info_ref, row_ref[...])
        kt_ref[...] = k_ref[...].astype(F32).T.astype(BF)

    allowed = [allowed_block(key_ref, pos_ref, c) for c in CHUNKS]
    weight = 1.0 / (1.0 + jnp.exp(-column(logit_ref[...])))
    slot = lax.broadcasted_iota(jnp.int32, (ROWS, 1), 0) + step * ROWS
    grad_o = jnp.where(slot < info_ref[1], go_ref[...], 0.0)
    grad_attn = (weight * grad_o).astype(BF)
    router = jnp.sum(grad_o * att_ref[...].astype(F32), axis=1, keepdims=True)
    router = jnp.broadcast_to(router, (ROWS, 128)).T[:1]
    lead = router.astype(BF).astype(F32)
    terms_ref[pl.ds(step, 1), :] = lead
    terms_ref[pl.ds(step + SLOTS // ROWS, 1), :] = router - lead
    for h in range(HEADS):
        lanes = slice(h * HEAD_SIZE, (h + 1) * HEAD_SIZE)
        q = q_ref[:, lanes]
        ga = grad_attn[:, lanes]
        lse = lse_ref[h : h + 1, :]
        p, gp, delta = [], [], jnp.zeros((1, ROWS), F32)
        for c, seen in zip(CHUNKS, allowed):
            s = rows_dot(k_ref[c : c + CHUNK, :], q) * SCALE
            p.append(jnp.exp(jnp.where(seen, s - lse, -1e30)))
            gp.append(rows_dot(v_ref[c : c + CHUNK, :], ga))
            delta = delta + jnp.sum(p[-1] * gp[-1], axis=0, keepdims=True)
        gs = [(a * (b - delta)).astype(BF) for a, b in zip(p, gp)]
        for c, a, b in zip(CHUNKS, gs, p):
            rows = slice(c, c + CHUNK)
            sum_ref[rows, :HEAD_SIZE] += jnp.dot(a, q, preferred_element_type=F32)
            sum_ref[rows, HEAD_SIZE:] += jnp.dot(b.astype(BF), ga, preferred_element_type=F32)
        gs = jnp.concatenate(gs, 0)
        gq = jnp.dot(kt_ref[...], gs, preferred_element_type=F32) * SCALE
        gq_ref[:, lanes] = gq.T.astype(BF)

    @pl.when(step == pl.num_programs(0) - 1)
    def _():
        core = info_ref[2]
        for ref, side in ((kept_ref, core), (sent_ref, 1 - core)):
            rows = pl.ds(pl.multiple_of(side * HALF, HALF), HALF)
            ref[:HALF, :HEAD_SIZE] = (sum_ref[rows, :HEAD_SIZE] * SCALE).astype(BF)
            ref[:HALF, HEAD_SIZE:] = sum_ref[rows, HEAD_SIZE:].astype(BF)
            ref[HALF:, :] = terms_ref[...].astype(BF)


def by_rows(width):
    return pl.BlockSpec((ROWS, width), lambda i, info: (i, 0))


def row_part():
    return pl.BlockSpec((1, ROWS), lambda i, info: (0, i))


def by_heads():
    return pl.BlockSpec((HEADS, ROWS), lambda i, info: (0, i))


def by_group():
    return pl.BlockSpec((SLOTS, HEAD_SIZE), lambda i, info: (0, info[0]))


def whole(shape):
    return pl.BlockSpec(shape, lambda i, info: (0,) * len(shape))


def shape_of(shape, dtype):
    return jax.ShapeDtypeStruct(shape, dtype)


def forward(info, q, k, v, pos_col, pos_row, logit_col):
    return pl.pallas_call(
        forward_kernel,
        grid_spec=pltpu.PrefetchScalarGridSpec(
            num_scalar_prefetch=1,
            grid=(SLOTS // ROWS,),
            in_specs=[by_rows(WIDE), by_group(), by_group(), row_part(), whole((1, SLOTS)), row_part()],
            out_specs=[by_rows(WIDE), pl.BlockSpec((WIDE, ROWS), lambda i, info: (0, i)), by_heads()],
            scratch_shapes=[pltpu.VMEM((SLOTS, ROWS), jnp.int32), pltpu.VMEM((HEAD_SIZE, SLOTS), BF)],
        ),
        out_shape=[shape_of((SLOTS, WIDE), BF), shape_of((WIDE, SLOTS), BF), shape_of((HEADS, SLOTS), F32)],
        compiler_params=SMALL,
        cost_estimate=pl.CostEstimate(flops=4 * 10**9, bytes_accessed=2 * 10**6, transcendentals=1200000),
    )(info, q, k, v, pos_col, pos_row, logit_col)


def backward(info, q, k, v, pos_col, pos_row, logit_col, lse, att, grad_o):
    return pl.pallas_call(
        backward_kernel,
        grid_spec=pltpu.PrefetchScalarGridSpec(
            num_scalar_prefetch=1,
            grid=(SLOTS // ROWS,),
            in_specs=[
                by_rows(WIDE), by_group(), by_group(), row_part(), whole((1, SLOTS)), row_part(),
                by_heads(), by_rows(WIDE), by_rows(WIDE),
            ],
            out_specs=[by_rows(WIDE), whole((HALF + EXTRA, WIDE)), whole((HALF + EXTRA, WIDE))],
            scratch_shapes=[
                pltpu.VMEM((SLOTS, WIDE), F32), pltpu.VMEM((EXTRA, WIDE), F32),
                pltpu.VMEM((SLOTS, ROWS), jnp.int32), pltpu.VMEM((HEAD_SIZE, SLOTS), BF),
            ],
        ),
        out_shape=[
            shape_of((SLOTS, WIDE), BF), shape_of((HALF + EXTRA, WIDE), BF),
            shape_of((HALF + EXTRA, WIDE), BF),
        ],
        compiler_params=LIMIT,
        cost_estimate=pl.CostEstimate(flops=7 * 10**9, bytes_accessed=4 * 10**6, transcendentals=1200000),
    )(info, q, k, v, pos_col, pos_row, logit_col, lse, att, grad_o)


def products_kernel(info_ref, near_ref, far_ref, w_ref, scaled_ref, *refs):
    go_ref, wg_ref = refs[-2:]
    core = info_ref[0]
    entry = [(info_ref[2] + info_ref[3] * s) % X for s in range(X)]
    w = [jnp.concatenate([w_ref[2 * s + core], w_ref[2 * s + 1 - core]], 0) for s in range(X)]
    for r in range(0, SLOTS, ROWS):
        rows = slice(r, r + ROWS)
        total = refs[0][rows] if len(refs) == 3 else jnp.zeros((ROWS, WIDE), F32)
        for s in range(X):
            both = jnp.concatenate([near_ref[entry[s], rows], far_ref[entry[s], rows]], 1)
            total = total + jnp.dot(both, w[s], preferred_element_type=F32)
        go_ref[rows] = total
    for s in range(X):
        for ref, y in ((near_ref, 2 * core), (far_ref, 2 - 2 * core)):
            grad = jnp.dot(scaled_ref[...], ref[entry[s]], preferred_element_type=F32).astype(BF)
            wg_ref[s % 2, y, s // 2] = grad[:, :128]
            wg_ref[s % 2, y + 1, s // 2] = grad[:, 128:]


def products(core, half, base, turn, near, far, w_out, scaled_t, begin=None):
    info = jnp.stack([core, half, base, turn]).astype(jnp.int32)
    more = [] if begin is None else [begin]
    shards = whole((X, SLOTS, WIDE))
    return pl.pallas_call(
        products_kernel,
        grid_spec=pltpu.PrefetchScalarGridSpec(
            num_scalar_prefetch=1,
            grid=(1,),
            in_specs=[
                shards, shards,
                pl.BlockSpec((X * CORE, WIDE, WIDE), lambda i, info: (info[1], 0, 0)),
                whole((WIDE, SLOTS)),
            ]
            + [whole((SLOTS, WIDE)) for _ in more],
            out_specs=[whole((SLOTS, WIDE)), whole((ZP, Y, 2, WIDE, 128))],
        ),
        out_shape=[shape_of((SLOTS, WIDE), F32), shape_of((ZP, Y, 2, WIDE, 128), BF)],
        compiler_params=LIMIT,
        cost_estimate=pl.CostEstimate(flops=2 * 10**10, bytes_accessed=8 * 10**6, transcendentals=0),
    )(info, near, far, w_out.reshape(ZH * X * CORE, WIDE, WIDE), scaled_t, *more)


def fold_kernel(info_ref, moved_ref, *refs):
    refs[-1][0] = jnp.sum(moved_ref[...].astype(F32), axis=0)[0].astype(BF)


def fold(half, moved, begin=None):
    more = [] if begin is None else [begin]
    return pl.pallas_call(
        fold_kernel,
        grid_spec=pltpu.PrefetchScalarGridSpec(
            num_scalar_prefetch=1,
            grid=(2,),
            in_specs=[pl.BlockSpec((ZP * Y, 1, WIDE, 128), lambda i, info: (0, i, 0, 0))]
            + [pl.BlockSpec(memory_space=pl.ANY) for _ in more],
            out_specs=pl.BlockSpec((1, WIDE, 128), lambda i, info: (info[0] * 2 + i, 0, 0)),
        ),
        out_shape=shape_of((ZQ, WIDE, 128), BF),
        input_output_aliases={2: 0} if more else {},
        compiler_params=SMALL,
        cost_estimate=pl.CostEstimate(flops=1 * 10**6, bytes_accessed=2 * 10**6, transcendentals=0),
    )(half.astype(jnp.int32).reshape(1), moved, *more)


def logits_kernel(router_ref, other_ref, logit_ref, out_ref):
    weight = 1.0 / (1.0 + jnp.exp(-logit_ref[...]))
    out_ref[...] = (router_ref[...] + other_ref[...]) * weight * (1.0 - weight)


def logits_gradient(router, other, logits):
    return pl.pallas_call(
        logits_kernel,
        out_shape=shape_of((1, SLOTS), F32),
        compiler_params=SMALL,
        cost_estimate=pl.CostEstimate(flops=2 * 10**10, bytes_accessed=10**4, transcendentals=0),
    )(router, other, logits)


def over_zp_y(blocks):
    blocks = blocks.reshape(ZP * Y, 2, WIDE, 128)
    return lax.all_to_all(blocks, ("zp", "y"), 0, 0, tiled=True)


def per_device(cotangent, routed, counts, logits, query_rows, key_rows, routed_value_rows, w_out):
    zh, x, core = lax.axis_index("zh"), lax.axis_index("x"), lax.axis_index("core")
    dp_index = (lax.axis_index("zq") * ZP + lax.axis_index("zp")) * Y + lax.axis_index("y")
    own = jnp.arange(counts.shape[0], dtype=jnp.int32) == dp_index
    own_count = jnp.sum(jnp.where(own, counts, 0))
    positions = routed[0]
    picked = cotangent[0].at[positions].get(mode="promise_in_bounds", wrap_negative_indices=False)
    picked = lax.optimization_barrier(picked)

    attention = (
        query_rows[0], key_rows[0], routed_value_rows[0],
        routed, routed, logits,
    )
    sizes = range(STEP, SLOTS + 1, STEP)
    branch = jnp.maximum(own_count - 1, 0) // STEP
    other, own_near, info, (attended, scaled_t, lse) = lax.switch(
        branch, [functools.partial(exchange, rows) for rows in sizes], picked, (x // 2, own_count, core), attention
    )
    other_near = jnp.stack([other] + [lax.ppermute(other, "x", ring(X, k)) for k in range(1, X)])
    own_far = swap(own_near, "core")
    begun, w_grad_own = products(core, zh, 0, 1, own_near, own_far, w_out, scaled_t)

    other_near, begun = lax.optimization_barrier((other_near, begun))
    other_far = swap(other_near, "core")
    moved_own = over_zp_y(w_grad_own)
    grad_o, w_grad_other = products(core, 1 - zh, x, 3, other_near, other_far, w_out, scaled_t, begun)

    moved_own, grad_o, w_grad_other = lax.optimization_barrier((moved_own, grad_o, w_grad_other))
    moved_other = over_zp_y(w_grad_other)
    blocks = fold(zh, moved_own)
    grad_q, kept, sent = backward(info, *attention, lse, attended, grad_o)
    came = swap(sent, "core")
    chip = (kept.astype(F32) + came.astype(F32)).astype(BF)

    moved_other, blocks, chip = lax.optimization_barrier((moved_other, blocks, chip))
    pair = lax.ppermute(chip, "x", [(0, 1), (1, 0), (2, 3), (3, 2)])
    blocks = fold(1 - zh, moved_other, blocks)
    pair, blocks = lax.optimization_barrier((pair, blocks))
    final = lax.all_to_all(blocks, "zq", 0, 0, tiled=True)
    w_grad = jnp.sum(final.astype(F32), axis=0).T.astype(BF)

    group = (chip.astype(F32) + pair.astype(F32)).astype(BF)
    apart = lax.ppermute(group, "x", [(0, 3), (3, 0), (1, 2), (2, 1)])
    router = group[HALF:].astype(F32) + apart[HALF:].astype(F32)
    router = (router[: SLOTS // WIDE] + router[SLOTS // WIDE : 2 * SLOTS // WIDE]).reshape(1, SLOTS)
    first = jnp.where(x < 2, group, apart)[:HALF]
    second = jnp.where(x < 2, apart, group)[:HALF]
    joined = jnp.concatenate(
        [first[:, :HEAD_SIZE], second[:, :HEAD_SIZE], first[:, HEAD_SIZE:], second[:, HEAD_SIZE:]], 1
    )
    theirs = swap(joined, "core")
    grad_logits = logits_gradient(router, swap(router, "zh"), logits)
    rows = jnp.where(
        core == 0, jnp.concatenate([joined, theirs], 0), jnp.concatenate([theirs, joined], 0)
    )
    key_total, value_total = rows[:, : 2 * HEAD_SIZE], rows[:, 2 * HEAD_SIZE :]
    return (grad_q[None], key_total[None], value_total[None], w_grad, grad_logits)


def solution(mesh):
    fine = Mesh(mesh.devices.reshape(ZQ, ZP, Y, ZH, X, CORE), ("zq", "zp", "y", "zh", "x", "core"))
    dp, col = ("zq", "zp", "y"), ("x", "core")
    row_col = ("zh",) + col
    placed = (
        P(dp, None, row_col),
        P(dp, None),
        P(),
        P(dp, None),
        P(dp, None, row_col),
        P(dp, None, "zh"),
        P(dp, None, "zh"),
        P(None, row_col),
    )
    return jax.shard_map(
        per_device,
        mesh=fine,
        in_specs=placed,
        out_specs=(
            P(dp, None, row_col),
            P(dp, None, "zh"),
            P(dp, None, "zh"),
            P(dp, row_col),
            P(dp, None),
        ),
        check_vma=False,
    )
```
